32 devices in a mesh: tm: 8 (over y, x, core), band: 4 (over z).
Axes of the slice: x: 2, y: 2, z: 4, core: 2. Of those that a mesh axis runs over, the one named last changes fastest.
Arguments:
- video: bfloat16 [8, 16, 104, 384], P('tm', 'band'), may hold values from -6 to 6
- past_first: bfloat16 [2, 16, 104, 384], P(None, 'band'), may hold values from -6 to 6
- past_second: bfloat16 [2, 16, 104, 384], P(None, 'band'), may hold values from -6 to 6
- conv_first: bfloat16 [3, 3, 3, 384, 384], P(None, None, None, 'tm'), may hold values from -0.0625 to 0.0625
- bias_first: float32 [384], replicated, may hold values from -3 to 3
- conv_second: bfloat16 [3, 3, 3, 384, 384], P(None, None, None, 'tm'), may hold values from -0.0625 to 0.0625
- bias_second: float32 [384], replicated, may hold values from -3 to 3
- gain_first: float32 [384], replicated, may hold values from 0.1 to 1.9
- gain_second: float32 [384], replicated, may hold values from 0.1 to 1.9
- gain_attn: float32 [384], replicated, may hold values from 0.1 to 1.9
- query_weight: bfloat16 [384, 384], replicated, may hold values from -1.5 to 4.5
- key_weight: bfloat16 [384, 384], replicated, may hold values from -1.5 to 4.5
- value_weight: bfloat16 [384, 384], replicated, may hold values from -0.3125 to 0.3125
- out_weight: bfloat16 [384, 384], replicated, may hold values from -0.3125 to 0.3125
Outputs:
- encoded: bfloat16 [8, 16, 104, 384], P('tm', 'band')
The draws below stay inside these ranges and needn't reach their ends.
All inputs are finite; a program needn't handle non-finite values.
Results may differ from the reference program's by a relative error of at most 0.012.
Values may be sent and summed in bfloat16 or wider, within the bound.
A program may use at most 128 MiB of HBM per device.

```python
import jax
import jax.numpy as jnp
from jax import lax

C = 384
W = 104
FRAMES = 8
HEIGHT = 16


def draw_query_weight(key, part):
    key = jax.random.fold_in(key, 11)
    sigma = jnp.sqrt(3.0 / C)
    matrix = jnp.clip(jax.random.normal(key, (C, C), jnp.float32) * sigma, -4.0 * sigma, 4.0 * sigma)
    return matrix.astype(jnp.bfloat16)


def draw_key_weight(key, part):
    key = jax.random.fold_in(key, 12)
    sigma = jnp.sqrt(3.0 / C)
    matrix = jnp.clip(jax.random.normal(key, (C, C), jnp.float32) * sigma, -4.0 * sigma, 4.0 * sigma)
    return matrix.astype(jnp.bfloat16)


def steps_of(key, dims, cuts, smallest, top_value):
    level, own = 1.0, jax.random.fold_in(key, 6)
    for position, shards_of in cuts:
        steps = jnp.exp(jax.random.uniform(jax.random.fold_in(own, position), (shards_of,), jnp.float32, smallest / len(cuts), top_value / len(cuts)))
        level = level * jnp.repeat(steps, dims[position] // shards_of).reshape([-1 if axis == position else 1 for axis in range(len(dims))])
    return level


def scatter_about(stream_key, shape, deviation, bound, split=(), kind=jnp.bfloat16):
    entries = jax.random.normal(stream_key, shape, jnp.float32) * deviation
    if len(split) > 0:
        entries = steps_of(stream_key, shape, split, -0.22, 0.18) * entries
    return jnp.clip(entries, min=-bound, max=bound).astype(kind)


def setup_inputs(seed: int = 0) -> dict:
    keys = jax.random.split(jax.random.key(seed), 15)
    video = scatter_about(keys[0], (FRAMES, HEIGHT, W, C), 1.0, 6.0, ((0, 8), (1, 4)))
    past_first = scatter_about(keys[1], (2, HEIGHT, W, C), 1.0, 6.0, ((1, 4),))
    past_second = scatter_about(keys[2], (2, HEIGHT, W, C), 1.0, 6.0, ((1, 4),))
    conv_first = scatter_about(keys[3], (3, 3, 3, C, C), (27 * C) ** -0.5, 0.0625, ((3, 8),))
    bias_first = scatter_about(keys[4], (C,), 0.5, 3.0, (), jnp.float32)
    conv_second = scatter_about(keys[5], (3, 3, 3, C, C), (27 * C) ** -0.5, 0.0625, ((3, 8),))
    bias_second = scatter_about(keys[6], (C,), 0.5, 3.0, (), jnp.float32)
    gain_first = jnp.clip(1.0 + 0.18 * jax.random.normal(keys[7], (C,), jnp.float32), 0.1, 1.9)
    gain_second = jnp.clip(1.0 + 0.18 * jax.random.normal(keys[8], (C,), jnp.float32), 0.1, 1.9)
    gain_attn = jnp.clip(1.0 + 0.18 * jax.random.normal(keys[9], (C,), jnp.float32), 0.1, 1.9)
    query_weight = draw_query_weight(jax.random.fold_in(keys[14], 71), 0)
    key_weight = draw_key_weight(jax.random.fold_in(keys[14], 71), 0)
    value_weight = scatter_about(keys[12], (C, C), C ** -0.5, 0.3125)
    out_weight = scatter_about(keys[13], (C, C), C ** -0.5, 0.3125)
    return dict(video=video, past_first=past_first, past_second=past_second, conv_first=conv_first, bias_first=bias_first, conv_second=conv_second, bias_second=bias_second, gain_first=gain_first, gain_second=gain_second, gain_attn=gain_attn, query_weight=query_weight, key_weight=key_weight, value_weight=value_weight, out_weight=out_weight)


def normalize(values_f32, gain):
    return values_f32 * lax.rsqrt(lax.optimization_barrier(jnp.mean(values_f32 * values_f32, axis=-1, keepdims=True)) + 1e-06) * gain

def causal_conv(sequence, kernel):
    result = lax.conv_general_dilated(sequence.astype(jnp.float32)[None], kernel.astype(jnp.float32), (1, 1, 1), ((0, 0), (1, 1), (1, 1)), dimension_numbers=('NDHWC', 'DHWIO', 'NDHWC'), precision=lax.Precision.HIGHEST)
    return result[0]

def reference(video, past_first, past_second, conv_first, bias_first, conv_second, bias_second, gain_first, gain_second, gain_attn, query_weight, key_weight, value_weight, out_weight):
    video_f32 = video.astype(jnp.float32)
    first_act = jax.nn.silu(normalize(video_f32, gain_first)).astype(jnp.bfloat16)
    hidden = causal_conv(jnp.concatenate([past_first, first_act], axis=0), conv_first) + bias_first
    second_act = jax.nn.silu(normalize(hidden, gain_second)).astype(jnp.bfloat16)
    conv_out = causal_conv(jnp.concatenate([past_second, second_act], axis=0), conv_second) + bias_second
    block_out = (video_f32 + conv_out).astype(jnp.bfloat16)
    frame_count, height, width, channels = block_out.shape
    normed = normalize(block_out.astype(jnp.float32), gain_attn).astype(jnp.bfloat16)
    normed = normed.reshape(frame_count, height * width, channels)
    factor = 1.0 / jnp.sqrt(jnp.float32(channels))

    def frame_attention(frame_tokens):
        queries = jnp.dot(frame_tokens, query_weight, preferred_element_type=jnp.float32).astype(jnp.bfloat16)
        key_rows = jnp.dot(frame_tokens, key_weight, preferred_element_type=jnp.float32).astype(jnp.bfloat16)
        value_rows = jnp.dot(frame_tokens, value_weight, preferred_element_type=jnp.float32).astype(jnp.bfloat16)
        scores = jnp.dot(queries, key_rows.T, preferred_element_type=jnp.float32) * factor
        top_score = lax.optimization_barrier(jnp.max(scores, axis=1, keepdims=True))
        expo = jnp.exp(scores - top_score)
        total = lax.optimization_barrier(jnp.sum(expo, axis=1, keepdims=True))
        mixed = jnp.dot(expo.astype(jnp.bfloat16), value_rows, preferred_element_type=jnp.float32)
        return (mixed / total).astype(jnp.bfloat16)
    att = lax.map(frame_attention, normed)
    att = att.reshape(frame_count * height * width, channels)
    projected = jnp.dot(att, out_weight, preferred_element_type=jnp.float32)
    projected = projected.reshape(frame_count, height, width, channels)
    return (block_out.astype(jnp.float32) + projected).astype(jnp.bfloat16)
```

```python
import functools

import jax
import jax.numpy as jnp
from jax import lax
from jax.experimental import pallas as pl
from jax.experimental.pallas import tpu as pltpu
from jax.sharding import PartitionSpec as P

MESH = pl.DeviceIdType.MESH
BF = jnp.bfloat16
F32 = jnp.float32
SLOT = 64
LANES = 2 * SLOT


def normalize(v, gain):
    return v * lax.rsqrt(jnp.mean(v * v, axis=-1, keepdims=True) + 1e-06) * gain


def silu(v):
    return v / (1.0 + jnp.exp(-v))


def kernel(
    chips, bands, rows, cols, wide,
    video, past1, past2, w1, w2, bias1, bias2, gain1, gain2, gain3, select,
    wq, wk, wv, wo, out,
    weights, stage, act, shifted, psend, precv, own, held, queries, top, total, accum,
    wl_sem, ws_sem, wr_sem, ms_sem, mr_sem, hs_sem, hr_sem, qs_sem, qr_sem,
    fs_sem, fr_sem, gs_sem, gr_sem, ps_sem, pr_sem, xr_sem, xright_sem, xleft_sem,
):
    t = lax.axis_index("tm")
    z = lax.axis_index("band")
    chip = t // 2
    core = t % 2
    mate = t + 1 - 2 * core
    last = bands - 1
    cells = rows * cols
    chans = video.shape[1]
    has_low = z > 0
    has_high = z < last

    def remote(src, dst, send, recv, tm, band):
        return pltpu.make_async_remote_copy(
            src_ref=src, dst_ref=dst, send_sem=send, recv_sem=recv,
            device_id=(tm, band), device_id_type=MESH,
        )

    def peer(d):
        return lax.rem(chip + d, chips)

    barrier = pltpu.get_barrier_semaphore()
    pl.semaphore_signal(barrier, inc=1, device_id=(mate, z), device_id_type=MESH)
    for d in range(1, chips):
        pl.semaphore_signal(barrier, inc=1, device_id=(peer(d) * 2 + core, z), device_id_type=MESH)

    @pl.when(has_low)
    def _():
        pl.semaphore_signal(barrier, inc=1, device_id=(t, z - 1), device_id_type=MESH)

    @pl.when(has_high)
    def _():
        pl.semaphore_signal(barrier, inc=1, device_id=(t, z + 1), device_id_type=MESH)

    def local_weight(conv, w):
        return pltpu.make_async_copy(w, weights.at[conv, :, core], wl_sem.at[conv])

    def sent_weight(conv, w):
        return remote(
            w, weights.at[conv, :, core], ws_sem.at[conv], wr_sem.at[conv], mate, z
        )

    def put_stage(conv, values):
        cube = values.reshape(rows, cols, chans)
        cube = jnp.concatenate([cube, jnp.zeros((rows, wide - cols, chans), F32)], axis=1)
        flat = cube.reshape(rows * wide, chans).astype(BF)
        spread = jnp.dot(flat, select[...], preferred_element_type=F32).astype(BF)
        for q in range(chips):
            stage[conv, q] = spread[:, q * LANES : (q + 1) * LANES].reshape(rows, wide, LANES)

    for conv, past in ((0, past1), (1, past2)):
        act[conv, 0, :, 1 : rows + 1] = past[...]

        @pl.when(z == 0)
        def _():
            act[conv, :, :, 0:1] = jnp.zeros((chips + 1, 2, 1, wide, LANES), BF)

        @pl.when(z == last)
        def _():
            act[conv, :, :, rows + 1 : rows + 2] = jnp.zeros((chips + 1, 2, 1, wide, LANES), BF)

    local_weight(0, w1).start()
    local_weight(1, w2).start()
    vid = video[...].astype(F32)
    put_stage(0, silu(normalize(vid, gain1[...])))
    act[0, chip + 1, core, 1 : rows + 1] = stage[0, chip]

    pl.semaphore_wait(
        barrier, chips + has_low.astype(jnp.int32) + has_high.astype(jnp.int32)
    )

    def main_copy(conv, d):
        q = peer(d)
        return remote(
            stage.at[conv, q], act.at[conv, chip + 1, core, pl.ds(1, rows)],
            ms_sem.at[conv, d], mr_sem.at[conv, d], q * 2 + core, z,
        )

    def past_up(conv):
        return remote(
            act.at[conv, 0, :, rows], act.at[conv, 0, :, 0],
            qs_sem.at[conv, 0], qr_sem.at[conv, 0], t, z + 1,
        )

    def past_down(conv):
        return remote(
            act.at[conv, 0, :, 1], act.at[conv, 0, :, rows + 1],
            qs_sem.at[conv, 1], qr_sem.at[conv, 1], t, z - 1,
        )

    def halo_up(conv):
        return remote(
            act.at[conv, pl.ds(1, chips), core, rows], act.at[conv, pl.ds(1, chips), core, 0],
            hs_sem.at[conv, 0], hr_sem.at[conv, 0], t, z + 1,
        )

    def halo_down(conv):
        return remote(
            act.at[conv, pl.ds(1, chips), core, 1],
            act.at[conv, pl.ds(1, chips), core, rows + 1],
            hs_sem.at[conv, 1], hr_sem.at[conv, 1], t, z - 1,
        )

    def give_main(conv, whose):
        part = act.at[conv, pl.ds(1, chips), whose, pl.ds(1, rows)]
        return remote(part, part, fs_sem.at[conv], fr_sem.at[conv], mate, z)

    def give_halo(conv, side, whose):
        part = act.at[conv, pl.ds(1, chips), whose, side * (rows + 1)]
        return remote(part, part, gs_sem.at[conv, side], gr_sem.at[conv, side], mate, z)

    def part_copy(conv, d):
        return remote(
            psend.at[conv, d - 1], precv.at[conv, d - 1],
            ps_sem.at[conv, d - 1], pr_sem.at[conv, d - 1], peer(d) * 2 + core, z,
        )

    def exchange(conv):
        for d in range(1, chips):
            main_copy(conv, d).start()
        if conv == 0:
            sent_weight(0, w1).start()
            for c in (0, 1):

                @pl.when(has_high)
                def _():
                    past_up(c).start()

                @pl.when(has_low)
                def _():
                    past_down(c).start()

        for d in range(1, chips):
            remote(
                stage.at[conv, 0],
                act.at[conv, lax.rem(chip + chips - d, chips) + 1, core, pl.ds(1, rows)],
                ms_sem.at[conv, d], mr_sem.at[conv, d], mate, z,
            ).wait_recv()

        @pl.when(has_high)
        def _():
            halo_up(conv).start()

        @pl.when(has_low)
        def _():
            halo_down(conv).start()

        give_main(conv, core).start()

        @pl.when(has_low)
        def _():
            halo_up(conv).wait_recv()
            give_halo(conv, 0, core).start()

        @pl.when(has_high)
        def _():
            halo_down(conv).wait_recv()
            give_halo(conv, 1, core).start()

        @pl.when(has_low)
        def _():
            past_up(conv).wait_recv()
            give_halo(conv, 0, 1 - core).wait_recv()

        @pl.when(has_high)
        def _():
            past_down(conv).wait_recv()
            give_halo(conv, 1, 1 - core).wait_recv()

        give_main(conv, 1 - core).wait_recv()

    def convolve(conv):
        def shift(n, _):
            flat = act[conv, n // 2, n % 2].reshape((rows + 2) * wide, LANES).astype(F32)
            size = (rows + 2) * wide
            shifted[0, n] = pltpu.roll(flat, 1, 0).astype(BF).reshape(rows + 2, wide, LANES)
            shifted[1, n] = pltpu.roll(flat, size - 1, 0).astype(BF).reshape(rows + 2, wide, LANES)
            return 0

        lax.fori_loop(0, 2 * (chips + 1), shift, 0)

        def frame(q):
            acc = jnp.zeros((rows * wide, chans), F32)
            for tap in range(3):
                n = 2 * q + core + tap
                pieces = []
                for r in range(3):
                    pieces.append(shifted[0, n, r : r + rows].reshape(rows * wide, LANES))
                    pieces.append(act[conv, n // 2, n % 2, r : r + rows].reshape(rows * wide, LANES))
                    pieces.append(shifted[1, n, r : r + rows].reshape(rows * wide, LANES))
                acc = acc + jnp.dot(
                    jnp.concatenate(pieces, axis=1),
                    weights[conv, 9 * tap : 9 * tap + 9].reshape(9 * LANES, chans),
                    preferred_element_type=F32,
                )
            return acc.reshape(rows, wide, chans)[:, :cols].reshape(cells, chans)

        def step(d, _):
            psend[conv, d - 1] = frame(peer(d)).astype(BF)
            part_copy(conv, d).start()
            return 0

        lax.fori_loop(1, chips, step, 0)
        own[...] = frame(chip)
        for d in range(1, chips):
            part_copy(conv, d).wait_recv()
            own[...] += precv[conv, d - 1].astype(F32)
        return own[...]

    exchange(0)
    sent_weight(1, w2).start()
    local_weight(0, w1).wait()
    remote(w1, weights.at[0, :, 1 - core], ws_sem.at[0], wr_sem.at[0], mate, z).wait_recv()
    hidden = convolve(0) + bias1[...]
    put_stage(1, silu(normalize(hidden, gain2[...])))
    act[1, chip + 1, core, 1 : rows + 1] = stage[1, chip]
    exchange(1)
    local_weight(1, w2).wait()
    remote(w2, weights.at[1, :, 1 - core], ws_sem.at[1], wr_sem.at[1], mate, z).wait_recv()
    block = (video[...].astype(F32) + (convolve(1) + bias2[...])).astype(BF)
    out[...] = block
    held[z] = normalize(block.astype(F32), gain3[...]).astype(BF)

    def right(b):
        return remote(held.at[b], held.at[b], xright_sem.at[b], xr_sem.at[b], t, z + 1)

    def left(b):
        return remote(held.at[b], held.at[b], xleft_sem.at[b], xr_sem.at[b], t, z - 1)

    @pl.when(has_high)
    def _():
        right(z).start()

    @pl.when(has_low)
    def _():
        left(z).start()

    factor = 1.0 / (float(chans) ** 0.5)
    queries[...] = jnp.dot(held[z], wq[...], preferred_element_type=F32).astype(BF)
    top[...] = jnp.full(top.shape, -jnp.inf, F32)
    total[...] = jnp.zeros(total.shape, F32)
    accum[...] = jnp.zeros(accum.shape, F32)

    def attend(b):
        tokens = held[b]
        keys = jnp.dot(tokens, wk[...], preferred_element_type=F32).astype(BF)
        values = jnp.dot(tokens, wv[...], preferred_element_type=F32).astype(BF)
        scores = lax.dot_general(
            queries[...], keys, (((1,), (1,)), ((), ())), preferred_element_type=F32
        ) * factor
        before = top[...]
        now = jnp.maximum(before, jnp.max(scores, axis=1, keepdims=True))
        shrink = jnp.exp(before - now)
        expo = jnp.exp(scores - now)
        top[...] = now
        total[...] = total[...] * shrink + jnp.sum(expo, axis=1, keepdims=True)
        accum[...] = accum[...] * shrink + jnp.dot(
            expo.astype(BF), values, preferred_element_type=F32
        )

    attend(z)

    def ring(k, _):
        @pl.when(z - k >= 0)
        def _():
            left_band = z - k
            right(left_band).wait_recv()

            @pl.when(has_high)
            def _():
                right(left_band).start()

        @pl.when(z + k < bands)
        def _():
            right_band = z + k
            left(right_band).wait_recv()

            @pl.when(has_low)
            def _():
                left(right_band).start()

        @pl.when(z - k >= 0)
        def _():
            attend(z - k)

        @pl.when(z + k < bands)
        def _():
            attend(z + k)

        return 0

    lax.fori_loop(1, bands, ring, 0)
    att = (accum[...] / total[...]).astype(BF)
    out[...] = (
        out[...].astype(F32) + jnp.dot(att, wo[...], preferred_element_type=F32)
    ).astype(BF)

    def drain(b, _):
        @pl.when(jnp.logical_and(has_high, b <= z))
        def _():
            right(b).wait_send()

        @pl.when(jnp.logical_and(has_low, b >= z))
        def _():
            left(b).wait_send()

        return 0

    lax.fori_loop(0, bands, drain, 0)
    for conv, w in ((0, w1), (1, w2)):
        sent_weight(conv, w).wait_send()
        give_main(conv, core).wait_send()
        for d in range(1, chips):
            main_copy(conv, d).wait_send()
            part_copy(conv, d).wait_send()

        @pl.when(has_high)
        def _():
            halo_up(conv).wait_send()
            past_up(conv).wait_send()
            give_halo(conv, 1, core).wait_send()

        @pl.when(has_low)
        def _():
            halo_down(conv).wait_send()
            past_down(conv).wait_send()
            give_halo(conv, 0, core).wait_send()


def local(
    devices, bands,
    video, past_first, past_second, conv_first, bias_first, conv_second, bias_second,
    gain_first, gain_second, gain_attn, query_weight, key_weight, value_weight, out_weight,
):
    _, rows, cols, chans = video.shape
    chips = devices // 2
    share = chans // devices
    wide = (cols + 1 + 15) // 16 * 16
    cells = rows * cols
    chip = lax.axis_index("tm") // 2

    def past_part(past):
        part = lax.dynamic_slice_in_dim(past, chip * 2 * share, 2 * share, axis=3)
        part = part.reshape(2, rows, cols, 2, share)
        part = jnp.pad(part, ((0, 0), (0, 0), (0, wide - cols), (0, 0), (0, SLOT - share)))
        return part.reshape(2, rows, wide, LANES)

    def weight_part(kernel_piece):
        flat = kernel_piece.reshape(27, share, chans)
        return jnp.pad(flat, ((0, 0), (0, SLOT - share), (0, 0)))

    channel = jnp.arange(chans)
    place = (channel // share) * SLOT + channel % share
    select = (place[:, None] == jnp.arange(chips * LANES)[None, :]).astype(BF)

    vmem = pl.BlockSpec(memory_space=pltpu.VMEM)
    hbm = pl.BlockSpec(memory_space=pl.ANY)
    dma = pltpu.SemaphoreType.DMA
    flops = 2 * 2 * cells * 27 * chans * chans + 4 * cells * cells * bands * chans
    row = lambda v: v.reshape(1, chans)
    encoded = pl.pallas_call(
        functools.partial(kernel, chips, bands, rows, cols, wide),
        out_shape=jax.ShapeDtypeStruct((cells, chans), BF),
        in_specs=[vmem] * 3 + [hbm] * 2 + [vmem] * 10,
        out_specs=vmem,
        scratch_shapes=[
            pltpu.VMEM((2, 27, 2, SLOT, chans), BF),
            pltpu.VMEM((2, chips, rows, wide, LANES), BF),
            pltpu.VMEM((2, chips + 1, 2, rows + 2, wide, LANES), BF),
            pltpu.VMEM((2, 2 * (chips + 1), rows + 2, wide, LANES), BF),
            pltpu.VMEM((2, chips - 1, cells, chans), BF),
            pltpu.VMEM((2, chips - 1, cells, chans), BF),
            pltpu.VMEM((cells, chans), F32),
            pltpu.VMEM((bands, cells, chans), BF),
            pltpu.VMEM((cells, chans), BF),
            pltpu.VMEM((cells, 1), F32),
            pltpu.VMEM((cells, 1), F32),
            pltpu.VMEM((cells, chans), F32),
            dma((2,)), dma((2,)), dma((2,)),
            dma((2, chips)), dma((2, chips)),
            dma((2, 2)), dma((2, 2)), dma((2, 2)), dma((2, 2)),
            dma((2,)), dma((2,)), dma((2, 2)), dma((2, 2)),
            dma((2, chips)), dma((2, chips)),
            dma((bands,)), dma((bands,)), dma((bands,)),
        ],
        compiler_params=pltpu.CompilerParams(
            collective_id=0, has_side_effects=True, vmem_limit_bytes=56 * 1024 * 1024
        ),
        cost_estimate=pl.CostEstimate(
            flops=flops, bytes_accessed=8 * 1024 * 1024, transcendentals=cells * cells * bands
        ),
    )(
        video.reshape(cells, chans), past_part(past_first), past_part(past_second),
        weight_part(conv_first), weight_part(conv_second),
        row(bias_first), row(bias_second), row(gain_first), row(gain_second), row(gain_attn),
        select, query_weight, key_weight, value_weight, out_weight,
    )
    return encoded.reshape(video.shape)


def solution(mesh):
    return jax.shard_map(
        functools.partial(local, mesh.shape["tm"], mesh.shape["band"]),
        mesh=mesh,
        in_specs=(
            P("tm", "band", None, None),
            P(None, "band", None, None),
            P(None, "band", None, None),
            P(None, None, None, "tm", None),
            P(),
            P(None, None, None, "tm", None),
            P(),
            P(),
            P(),
            P(),
            P(),
            P(),
            P(),
            P(),
        ),
        out_specs=P("tm", "band", None, None),
        check_vma=False,
    )
```

```python
import functools

import jax
import jax.numpy as jnp
from jax import lax
from jax.experimental import pallas as pl
from jax.experimental.pallas import tpu as pltpu
from jax.sharding import PartitionSpec as P

MESH = pl.DeviceIdType.MESH
BF = jnp.bfloat16
F32 = jnp.float32
SLOT = 64
LANES = 2 * SLOT


def normalize(v, gain):
    return v * lax.rsqrt(jnp.mean(v * v, axis=-1, keepdims=True) + 1e-06) * gain


def silu(v):
    return v / (1.0 + jnp.exp(-v))


def kernel(
    chips, bands, rows, cols, wide,
    share, direct,
    video, past1, past2, w1, w2, bias1, bias2, gain1, gain2, gain3,
    wq, wk, wv, wo, out,
    weights, stage, act, shifted, psend, precv, work, kept, held, queries, top, total, accum,
    wl_sem, ws_sem, wr_sem, ms_sem, mr_sem, hs_sem, hr_sem, qs_sem, qr_sem,
    fs_sem, fr_sem, gs_sem, gr_sem, ps_sem, pr_sem, xr_sem, xright_sem, xleft_sem,
):
    t = lax.axis_index("tm")
    z = lax.axis_index("band")
    chip = t // 2
    core = t % 2
    mate = t + 1 - 2 * core
    last = bands - 1
    plane = chips == 4 and rows % 4 == 0
    cells = rows * cols
    half = rows // 2
    chans = video.shape[1]
    has_low = z > 0
    has_high = z < last

    def remote(src, dst, send, recv, tm, band):
        return pltpu.make_async_remote_copy(
            src_ref=src, dst_ref=dst, send_sem=send, recv_sem=recv,
            device_id=(tm, band), device_id_type=MESH,
        )

    def peer(d):
        return lax.rem(chip + d, chips)

    barrier = pltpu.get_barrier_semaphore()
    pl.semaphore_signal(barrier, inc=1, device_id=(mate, z), device_id_type=MESH)
    for d in range(1, chips):
        pl.semaphore_signal(barrier, inc=1, device_id=(peer(d) * 2 + core, z), device_id_type=MESH)

    @pl.when(has_low)
    def _():
        pl.semaphore_signal(barrier, inc=1, device_id=(t, z - 1), device_id_type=MESH)

    @pl.when(has_high)
    def _():
        pl.semaphore_signal(barrier, inc=1, device_id=(t, z + 1), device_id_type=MESH)

    def weight_slot(conv, whose):
        slot = weights.at[conv, :, whose]
        return slot.at[:, pl.ds(0, share)] if direct else slot

    def local_weight(conv, w):
        return pltpu.make_async_copy(w, weight_slot(conv, core), wl_sem.at[conv])

    def sent_weight(conv, w):
        return remote(
            w, weight_slot(conv, core), ws_sem.at[conv], wr_sem.at[conv], mate, z
        )

    def spread_of(values, first, count):
        lead = values.shape[0] // cols
        cube = values.reshape(lead, cols, chans)
        cube = jnp.concatenate([cube, jnp.zeros((lead, wide - cols, chans), F32)], axis=1)
        flat = cube.reshape(lead * wide, chans).astype(BF)
        channel = lax.broadcasted_iota(jnp.int32, (chans, count * LANES), 0)
        lane = lax.broadcasted_iota(jnp.int32, (chans, count * LANES), 1)
        within = lane % SLOT
        source = (lane // SLOT + 2 * first) * share + within
        chosen = jnp.logical_and(channel == source, within < share)
        select = jnp.where(chosen, 1.0, 0.0).astype(BF)
        return jnp.dot(flat, select, preferred_element_type=F32).astype(BF)

    def put_stage(conv, h, values):
        spread = spread_of(values, 0, chips)
        mine = pl.ds(h * half, half)
        for q in range(chips):
            stage[conv, q, mine] = spread[:, q * LANES : (q + 1) * LANES].reshape(
                half, wide, LANES
            )
        act[conv, chip + 1, core, pl.ds(1 + h * half, half)] = stage[conv, chip, mine]

    def fill_past():
        for conv, past in ((0, past1), (1, past2)):
            for n in range(2):
                part = spread_of(past[n].reshape(cells, chans).astype(F32), chip, 1)
                act[conv, 0, n, 1 : rows + 1] = part.reshape(rows, wide, LANES)
            if direct:
                weights[conv, :, :, share:] = jnp.zeros((27, 2, SLOT - share, chans), BF)

            @pl.when(z == 0)
            def _():
                act[conv, :, :, 0:1] = jnp.zeros((chips + 1, 2, 1, wide, LANES), BF)

            @pl.when(z == last)
            def _():
                act[conv, :, :, rows + 1 : rows + 2] = jnp.zeros((chips + 1, 2, 1, wide, LANES), BF)

    local_weight(0, w1).start()
    local_weight(1, w2).start()
    vid = video[...].astype(F32)
    active = silu(normalize(vid, gain1[...].reshape(1, chans)))
    for h in range(2):
        put_stage(0, h, active[h * half * cols : (h + 1) * half * cols])

    pl.semaphore_wait(
        barrier, chips + has_low.astype(jnp.int32) + has_high.astype(jnp.int32)
    )

    def main_copy(conv, d, h):
        q = peer(d)
        return remote(
            stage.at[conv, q, pl.ds(h * half, half)],
            act.at[conv, chip + 1, core, pl.ds(1 + h * half, half)],
            ms_sem.at[conv, d, h], mr_sem.at[conv, d, h], q * 2 + core, z,
        )

    def main_came(conv, d, h):
        source = lax.rem(chip + chips - d, chips)
        return remote(
            stage.at[conv, 0, pl.ds(h * half, half)],
            act.at[conv, source + 1, core, pl.ds(1 + h * half, half)],
            ms_sem.at[conv, d, h], mr_sem.at[conv, d, h], mate, z,
        )

    def past_up(conv):
        return remote(
            act.at[conv, 0, :, rows], act.at[conv, 0, :, 0],
            qs_sem.at[conv, 0], qr_sem.at[conv, 0], t, z + 1,
        )

    def past_down(conv):
        return remote(
            act.at[conv, 0, :, 1], act.at[conv, 0, :, rows + 1],
            qs_sem.at[conv, 1], qr_sem.at[conv, 1], t, z - 1,
        )

    def halo_up(conv):
        return remote(
            act.at[conv, pl.ds(1, chips), core, rows], act.at[conv, pl.ds(1, chips), core, 0],
            hs_sem.at[conv, 0], hr_sem.at[conv, 0], t, z + 1,
        )

    def halo_down(conv):
        return remote(
            act.at[conv, pl.ds(1, chips), core, 1],
            act.at[conv, pl.ds(1, chips), core, rows + 1],
            hs_sem.at[conv, 1], hr_sem.at[conv, 1], t, z - 1,
        )

    def give_main(conv, whose):
        part = act.at[conv, pl.ds(1, chips), whose, pl.ds(1, rows)]
        return remote(part, part, fs_sem.at[conv], fr_sem.at[conv], mate, z)

    def give_halo(conv, side, whose):
        part = act.at[conv, pl.ds(1, chips), whose, side * (rows + 1)]
        return remote(part, part, gs_sem.at[conv, side], gr_sem.at[conv, side], mate, z)

    def part_copy(conv, d):
        return remote(
            psend.at[conv, d - 1], precv.at[conv, d - 1],
            ps_sem.at[conv, d - 1, 0], pr_sem.at[conv, d - 1, 0], peer(d) * 2 + core, z,
        )

    across = chip + 1 - 2 * (chip % 2)
    along = chip + 2 - 4 * (chip // 2)

    def row_copy(conv, kind, r):
        first, second = (across, along) if r % 2 == 0 else (along, across)
        target = second if kind == 2 else first
        return remote(
            psend.at[conv, kind, r], precv.at[conv, kind, r],
            ps_sem.at[conv, kind, r], pr_sem.at[conv, kind, r], target * 2 + core, z,
        )

    def exchange(conv):
        if conv == 0:
            sent_weight(0, w1).start()
            for h in range(2):
                for d in range(1, chips):
                    main_copy(conv, d, h).start()
            fill_past()
            for c in (0, 1):

                @pl.when(has_high)
                def _():
                    past_up(c).start()

                @pl.when(has_low)
                def _():
                    past_down(c).start()

        for d in range(1, chips):
            main_came(conv, d, 0).wait_recv()

        @pl.when(has_low)
        def _():
            halo_down(conv).start()

        for d in range(1, chips):
            main_came(conv, d, 1).wait_recv()

        @pl.when(has_high)
        def _():
            halo_up(conv).start()

        give_main(conv, core).start()

        @pl.when(has_low)
        def _():
            halo_up(conv).wait_recv()
            give_halo(conv, 0, core).start()

        @pl.when(has_high)
        def _():
            halo_down(conv).wait_recv()
            give_halo(conv, 1, core).start()

        @pl.when(has_low)
        def _():
            past_up(conv).wait_recv()
            give_halo(conv, 0, 1 - core).wait_recv()

        @pl.when(has_high)
        def _():
            past_down(conv).wait_recv()
            give_halo(conv, 1, 1 - core).wait_recv()

        give_main(conv, 1 - core).wait_recv()

    def convolve(conv, consume):
        def shift(n, _):
            flat = act[conv, n // 2, n % 2].reshape((rows + 2) * wide, LANES).astype(F32)
            size = (rows + 2) * wide
            shifted[0, n] = pltpu.roll(flat, 1, 0).astype(BF).reshape(rows + 2, wide, LANES)
            shifted[1, n] = pltpu.roll(flat, size - 1, 0).astype(BF).reshape(rows + 2, wide, LANES)
            return 0

        lax.fori_loop(0, 2 * (chips + 1), shift, 0)

        def frame(q):
            acc = jnp.zeros((rows * wide, chans), F32)
            for tap in range(3):
                n = 2 * q + core + tap
                pieces = []
                for r in range(3):
                    pieces.append(shifted[0, n, r : r + rows].reshape(rows * wide, LANES))
                    pieces.append(act[conv, n // 2, n % 2, r : r + rows].reshape(rows * wide, LANES))
                    pieces.append(shifted[1, n, r : r + rows].reshape(rows * wide, LANES))
                acc = acc + jnp.dot(
                    jnp.concatenate(pieces, axis=1),
                    weights[conv, 9 * tap : 9 * tap + 9].reshape(9 * LANES, chans),
                    preferred_element_type=F32,
                )
            work[...] = acc.reshape(rows, wide, chans)[:, :cols]

        def sum_row(r):
            row_copy(conv, 0, r).wait_recv()
            psend[conv, 2, r] = (kept[r] + precv[conv, 0, r].astype(F32)).astype(BF)
            row_copy(conv, 2, r).start()

        def plane_step(i, _):
            x = (chip + 1 - i // 2) % 2
            y = (chip // 2 + 1 - i % 2) % 2
            frame(2 * y + x)

            @pl.when(i == 0)
            def _():
                for r in range(rows):
                    psend[conv, 0, r] = work[r].astype(BF)
                    row_copy(conv, 0, r).start()

            @pl.when(i == 1)
            def _():
                for r in range(0, rows, 2):
                    psend[conv, 1, r] = work[r].astype(BF)
                    if r < half:
                        row_copy(conv, 1, r).start()
                    kept[r + 1] = work[r + 1]

            @pl.when(i == 2)
            def _():
                for r in range(0, rows, 2):
                    psend[conv, 1, r + 1] = work[r + 1].astype(BF)
                    if r + 1 < half:
                        row_copy(conv, 1, r + 1).start()
                    kept[r] = work[r]
                for r in range(half):
                    sum_row(r)
                for r in range(half, rows):
                    row_copy(conv, 1, r).start()

            return 0

        def step(d, _):
            frame(peer(d))
            psend[conv, d - 1] = work[...].astype(BF)
            part_copy(conv, d).start()
            return 0

        if plane:
            lax.fori_loop(0, 4, plane_step, 0)
            for r in range(half, rows):
                sum_row(r)
        else:
            lax.fori_loop(1, chips, step, 0)
            frame(chip)
            for d in range(1, chips):
                part_copy(conv, d).wait_recv()
        for h in range(2):
            mine = slice(h * half, (h + 1) * half)
            for kind in range(1 if plane else 0, chips - 1):
                if plane:
                    for r in range(h * half, (h + 1) * half):
                        row_copy(conv, kind, r).wait_recv()
                work[mine] += precv[conv, kind, mine].astype(F32)
            consume(h, work[mine].reshape(half * cols, chans))

    exchange(0)
    sent_weight(1, w2).start()
    local_weight(0, w1).wait()
    remote(w1, weight_slot(0, 1 - core), ws_sem.at[0], wr_sem.at[0], mate, z).wait_recv()

    def after_first(h, summed):
        hidden = summed + bias1[...].reshape(1, chans)
        put_stage(1, h, silu(normalize(hidden, gain2[...].reshape(1, chans))))
        for d in range(1, chips):
            main_copy(1, d, h).start()

    convolve(0, after_first)
    exchange(1)
    local_weight(1, w2).wait()
    remote(w2, weight_slot(1, 1 - core), ws_sem.at[1], wr_sem.at[1], mate, z).wait_recv()

    def right(b, h):
        return remote(
            held.at[b, h], held.at[b, h], xright_sem.at[b, h], xr_sem.at[b, h], t, z + 1
        )

    def left(b, h):
        return remote(
            held.at[b, h], held.at[b, h], xleft_sem.at[b, h], xr_sem.at[b, h], t, z - 1
        )

    def after_second(h, summed):
        mine = slice(h * half * cols, (h + 1) * half * cols)
        conv_out = summed + bias2[...].reshape(1, chans)
        block = (video[mine].astype(F32) + conv_out).astype(BF)
        out[mine] = block
        held[z, h] = normalize(block.astype(F32), gain3[...].reshape(1, chans)).astype(BF)

        @pl.when(has_high)
        def _():
            right(z, h).start()

        @pl.when(has_low)
        def _():
            left(z, h).start()

    convolve(1, after_second)
    factor = 1.0 / (float(chans) ** 0.5)
    queries[...] = jnp.dot(held[z].reshape(cells, chans), wq[...], preferred_element_type=F32).astype(BF)
    top[...] = jnp.full(top.shape, -jnp.inf, F32)
    total[...] = jnp.zeros(total.shape, F32)
    accum[...] = jnp.zeros(accum.shape, F32)

    def attend(b):
        tokens = held[b].reshape(cells, chans)
        keys = jnp.dot(tokens, wk[...], preferred_element_type=F32).astype(BF)
        values = jnp.dot(tokens, wv[...], preferred_element_type=F32).astype(BF)
        scores = lax.dot_general(
            queries[...], keys, (((1,), (1,)), ((), ())), preferred_element_type=F32
        ) * factor
        before = top[...]
        now = jnp.maximum(before, jnp.max(scores, axis=1, keepdims=True))
        shrink = jnp.exp(before - now)
        expo = jnp.exp(scores - now)
        top[...] = now
        total[...] = total[...] * shrink + jnp.sum(expo, axis=1, keepdims=True)
        accum[...] = accum[...] * shrink + jnp.dot(
            expo.astype(BF), values, preferred_element_type=F32
        )

    attend(z)

    def ring(k, _):
        for h in range(2):

            @pl.when(z - k >= 0)
            def _():
                right(z - k, h).wait_recv()

                @pl.when(has_high)
                def _():
                    right(z - k, h).start()

            @pl.when(z + k < bands)
            def _():
                left(z + k, h).wait_recv()

                @pl.when(has_low)
                def _():
                    left(z + k, h).start()

        @pl.when(z - k >= 0)
        def _():
            attend(z - k)

        @pl.when(z + k < bands)
        def _():
            attend(z + k)

        return 0

    lax.fori_loop(1, bands, ring, 0)
    att = (accum[...] / total[...]).astype(BF)
    out[...] = (
        out[...].astype(F32) + jnp.dot(att, wo[...], preferred_element_type=F32)
    ).astype(BF)

    def drain(b, _):
        @pl.when(jnp.logical_and(has_high, b <= z))
        def _():
            for h in range(2):
                right(b, h).wait_send()

        @pl.when(jnp.logical_and(has_low, b >= z))
        def _():
            for h in range(2):
                left(b, h).wait_send()

        return 0

    lax.fori_loop(0, bands, drain, 0)
    for conv, w in ((0, w1), (1, w2)):
        sent_weight(conv, w).wait_send()
        give_main(conv, core).wait_send()
        for d in range(1, chips):
            for h in range(2):
                main_copy(conv, d, h).wait_send()
            if plane:
                for r in range(rows):
                    row_copy(conv, d - 1, r).wait_send()
            else:
                part_copy(conv, d).wait_send()

        @pl.when(has_high)
        def _():
            halo_up(conv).wait_send()
            past_up(conv).wait_send()
            give_halo(conv, 1, core).wait_send()

        @pl.when(has_low)
        def _():
            halo_down(conv).wait_send()
            past_down(conv).wait_send()
            give_halo(conv, 0, core).wait_send()


def local(
    devices, bands,
    video, past_first, past_second, conv_first, bias_first, conv_second, bias_second,
    gain_first, gain_second, gain_attn, query_weight, key_weight, value_weight, out_weight,
):
    _, rows, cols, chans = video.shape
    chips = devices // 2
    share = chans // devices
    wide = (cols + 1 + 15) // 16 * 16
    cells = rows * cols
    direct = share % 16 == 0 and share < SLOT

    def weight_part(kernel_piece):
        flat = kernel_piece.reshape(27, share, chans)
        if direct:
            return flat
        return jnp.pad(flat, ((0, 0), (0, SLOT - share), (0, 0)))

    vmem = pl.BlockSpec(memory_space=pltpu.VMEM)
    hbm = pl.BlockSpec(memory_space=pl.ANY)
    dma = pltpu.SemaphoreType.DMA
    flops = 2 * 2 * cells * 27 * chans * chans + 4 * cells * cells * bands * chans
    encoded = pl.pallas_call(
        functools.partial(kernel, chips, bands, rows, cols, wide, share, direct),
        out_shape=jax.ShapeDtypeStruct((cells, chans), BF),
        in_specs=[vmem] * 3 + [hbm] * 2 + [vmem] * 9,
        out_specs=vmem,
        scratch_shapes=[
            pltpu.VMEM((2, 27, 2, SLOT, chans), BF),
            pltpu.VMEM((2, chips, rows, wide, LANES), BF),
            pltpu.VMEM((2, chips + 1, 2, rows + 2, wide, LANES), BF),
            pltpu.VMEM((2, 2 * (chips + 1), rows + 2, wide, LANES), BF),
            pltpu.VMEM((2, chips - 1, rows, cols, chans), BF),
            pltpu.VMEM((2, chips - 1, rows, cols, chans), BF),
            pltpu.VMEM((rows, cols, chans), F32),
            pltpu.VMEM((rows, cols, chans), F32),
            pltpu.VMEM((bands, 2, cells // 2, chans), BF),
            pltpu.VMEM((cells, chans), BF),
            pltpu.VMEM((cells, 1), F32),
            pltpu.VMEM((cells, 1), F32),
            pltpu.VMEM((cells, chans), F32),
            dma((2,)), dma((2,)), dma((2,)),
            dma((2, chips, 2)), dma((2, chips, 2)),
            dma((2, 2)), dma((2, 2)), dma((2, 2)), dma((2, 2)),
            dma((2,)), dma((2,)), dma((2, 2)), dma((2, 2)),
            dma((2, chips, rows)), dma((2, chips, rows)),
            dma((bands, 2)), dma((bands, 2)), dma((bands, 2)),
        ],
        compiler_params=pltpu.CompilerParams(
            collective_id=0, has_side_effects=True, vmem_limit_bytes=56 * 1024 * 1024
        ),
        cost_estimate=pl.CostEstimate(
            flops=flops, bytes_accessed=8 * 1024 * 1024, transcendentals=cells * cells * bands
        ),
    )(
        video.reshape(cells, chans), past_first, past_second,
        weight_part(conv_first), weight_part(conv_second),
        bias_first, bias_second, gain_first, gain_second, gain_attn,
        query_weight, key_weight, value_weight, out_weight,
    )
    return encoded.reshape(video.shape)


def solution(mesh):
    return jax.shard_map(
        functools.partial(local, mesh.shape["tm"], mesh.shape["band"]),
        mesh=mesh,
        in_specs=(
            P("tm", "band", None, None),
            P(None, "band", None, None),
            P(None, "band", None, None),
            P(None, None, None, "tm", None),
            P(),
            P(None, None, None, "tm", None),
            P(),
            P(),
            P(),
            P(),
            P(),
            P(),
            P(),
            P(),
        ),
        out_specs=P("tm", "band", None, None),
        check_vma=False,
    )
```

```python
import functools

import jax
import jax.numpy as jnp
from jax import lax
from jax.experimental import pallas as pl
from jax.experimental.pallas import tpu as pltpu
from jax.sharding import PartitionSpec as P

MESH = pl.DeviceIdType.MESH
BF = jnp.bfloat16
F32 = jnp.float32
SLOT = 64
LANES = 2 * SLOT
GROUPS = ((1, 2), (0, 3))
PIECES = ((1, 2), (0, 1), (3, 1))


def normalize(v, gain):
    return v * lax.rsqrt(jnp.mean(v * v, axis=-1, keepdims=True) + 1e-06) * gain


def silu(v):
    return v / (1.0 + jnp.exp(-v))


def kernel(
    chips, bands, rows, cols, wide,
    share, direct,
    video, past1, past2, w1, w2, bias1, bias2, gain1, gain2, gain3,
    wq, wk, wv, wo, out,
    weights, stage, act, shifted, psend, precv, work, kept, held, queries, top, total, accum,
    wl_sem, ws_sem, wr_sem, ms_sem, mr_sem, hs_sem, hr_sem, qs_sem, qr_sem,
    fs_sem, fr_sem, gs_sem, gr_sem, ps_sem, pr_sem, xr_sem, xright_sem, xleft_sem,
):
    t = lax.axis_index("tm")
    z = lax.axis_index("band")
    chip = t // 2
    core = t % 2
    mate = t + 1 - 2 * core
    last = bands - 1
    plane = chips == 4
    cells = rows * cols
    chans = video.shape[1]
    has_low = z > 0
    has_high = z < last

    def remote(src, dst, send, recv, tm, band):
        return pltpu.make_async_remote_copy(
            src_ref=src, dst_ref=dst, send_sem=send, recv_sem=recv,
            device_id=(tm, band), device_id_type=MESH,
        )

    def peer(d):
        return lax.rem(chip + d, chips)

    barrier = pltpu.get_barrier_semaphore()
    pl.semaphore_signal(barrier, inc=1, device_id=(mate, z), device_id_type=MESH)
    for d in range(1, chips):
        pl.semaphore_signal(barrier, inc=1, device_id=(peer(d) * 2 + core, z), device_id_type=MESH)

    @pl.when(has_low)
    def _():
        pl.semaphore_signal(barrier, inc=1, device_id=(t, z - 1), device_id_type=MESH)

    @pl.when(has_high)
    def _():
        pl.semaphore_signal(barrier, inc=1, device_id=(t, z + 1), device_id_type=MESH)

    def weight_slot(conv, whose):
        slot = weights.at[conv, :, whose]
        return slot.at[:, pl.ds(0, share)] if direct else slot

    def local_weight(conv, w):
        return pltpu.make_async_copy(w, weight_slot(conv, core), wl_sem.at[conv])

    def sent_weight(conv, w):
        return remote(
            w, weight_slot(conv, core), ws_sem.at[conv], wr_sem.at[conv], mate, z
        )

    def spread_of(values, first, count):
        lead = values.shape[0] // cols
        cube = values.reshape(lead, cols, chans)
        cube = jnp.concatenate([cube, jnp.zeros((lead, wide - cols, chans), F32)], axis=1)
        flat = cube.reshape(lead * wide, chans).astype(BF)
        channel = lax.broadcasted_iota(jnp.int32, (chans, count * LANES), 0)
        lane = lax.broadcasted_iota(jnp.int32, (chans, count * LANES), 1)
        within = lane % SLOT
        source = (lane // SLOT + 2 * first) * share + within
        chosen = jnp.logical_and(channel == source, within < share)
        select = jnp.where(chosen, 1.0, 0.0).astype(BF)
        return jnp.dot(flat, select, preferred_element_type=F32).astype(BF)

    def put_stage(conv, g, values):
        spread = spread_of(values, 0, chips)
        for i, r in enumerate(GROUPS[g]):
            for q in range(chips):
                stage[conv, q, r] = spread[i * wide : (i + 1) * wide, q * LANES : (q + 1) * LANES]
            act[conv, chip + 1, core, r + 1] = stage[conv, chip, r]

    def rows_of(cube, g):
        first, second = GROUPS[g]
        return jnp.concatenate([cube[first], cube[second]], axis=0)

    def fill_past():
        for conv, past in ((0, past1), (1, past2)):
            for n in range(2):
                part = spread_of(past[n].reshape(cells, chans).astype(F32), chip, 1)
                act[conv, 0, n, 1 : rows + 1] = part.reshape(rows, wide, LANES)
            if direct:
                weights[conv, :, :, share:] = jnp.zeros((27, 2, SLOT - share, chans), BF)

            @pl.when(z == 0)
            def _():
                act[conv, :, :, 0:1] = jnp.zeros((chips + 1, 2, 1, wide, LANES), BF)

            @pl.when(z == last)
            def _():
                act[conv, :, :, rows + 1 : rows + 2] = jnp.zeros((chips + 1, 2, 1, wide, LANES), BF)

    local_weight(0, w1).start()
    local_weight(1, w2).start()
    vid = video[...].astype(F32).reshape(rows, cols, chans)
    for g in range(2):
        put_stage(0, g, silu(normalize(rows_of(vid, g), gain1[...].reshape(1, chans))))

    pl.semaphore_wait(
        barrier, chips + has_low.astype(jnp.int32) + has_high.astype(jnp.int32)
    )

    def main_copy(conv, d, piece):
        q = peer(d)
        first, count = PIECES[piece]
        return remote(
            stage.at[conv, q, pl.ds(first, count)],
            act.at[conv, chip + 1, core, pl.ds(first + 1, count)],
            ms_sem.at[conv, d, piece], mr_sem.at[conv, d, piece], q * 2 + core, z,
        )

    def main_came(conv, d, piece):
        source = lax.rem(chip + chips - d, chips)
        first, count = PIECES[piece]
        return remote(
            stage.at[conv, 0, pl.ds(first, count)],
            act.at[conv, source + 1, core, pl.ds(first + 1, count)],
            ms_sem.at[conv, d, piece], mr_sem.at[conv, d, piece], mate, z,
        )

    def past_up(conv):
        return remote(
            act.at[conv, 0, :, rows], act.at[conv, 0, :, 0],
            qs_sem.at[conv, 0], qr_sem.at[conv, 0], t, z + 1,
        )

    def past_down(conv):
        return remote(
            act.at[conv, 0, :, 1], act.at[conv, 0, :, rows + 1],
            qs_sem.at[conv, 1], qr_sem.at[conv, 1], t, z - 1,
        )

    def halo_up(conv):
        return remote(
            act.at[conv, pl.ds(1, chips), core, rows], act.at[conv, pl.ds(1, chips), core, 0],
            hs_sem.at[conv, 0], hr_sem.at[conv, 0], t, z + 1,
        )

    def halo_down(conv):
        return remote(
            act.at[conv, pl.ds(1, chips), core, 1],
            act.at[conv, pl.ds(1, chips), core, rows + 1],
            hs_sem.at[conv, 1], hr_sem.at[conv, 1], t, z - 1,
        )

    def give_main(conv, whose):
        part = act.at[conv, pl.ds(1, chips), whose, pl.ds(1, rows)]
        return remote(part, part, fs_sem.at[conv], fr_sem.at[conv], mate, z)

    def give_halo(conv, side, whose):
        part = act.at[conv, pl.ds(1, chips), whose, side * (rows + 1)]
        return remote(part, part, gs_sem.at[conv, side], gr_sem.at[conv, side], mate, z)

    def part_copy(conv, d):
        return remote(
            psend.at[conv, d - 1], precv.at[conv, d - 1],
            ps_sem.at[conv, d - 1, 0], pr_sem.at[conv, d - 1, 0], peer(d) * 2 + core, z,
        )

    across = chip + 1 - 2 * (chip % 2)
    along = chip + 2 - 4 * (chip // 2)

    def row_copy(conv, kind, r):
        first, second = (across, along) if r % 2 == 0 else (along, across)
        target = second if kind == 2 else first
        return remote(
            psend.at[conv, kind, r], precv.at[conv, kind, r],
            ps_sem.at[conv, kind, r], pr_sem.at[conv, kind, r], target * 2 + core, z,
        )

    def exchange(conv):
        if conv == 0:
            sent_weight(0, w1).start()
            for piece in range(3):
                for d in range(1, chips):
                    main_copy(conv, d, piece).start()
            fill_past()
            for c in (0, 1):

                @pl.when(has_high)
                def _():
                    past_up(c).start()

                @pl.when(has_low)
                def _():
                    past_down(c).start()

        for piece in (1, 2, 0):
            for d in range(1, chips):
                main_came(conv, d, piece).wait_recv()

        give_main(conv, core).start()

        @pl.when(has_low)
        def _():
            halo_down(conv).start()

        @pl.when(has_high)
        def _():
            halo_up(conv).start()

        give_main(conv, 1 - core).wait_recv()

    def pass_halo(conv):
        @pl.when(has_low)
        def _():
            halo_up(conv).wait_recv()
            give_halo(conv, 0, core).start()

        @pl.when(has_high)
        def _():
            halo_down(conv).wait_recv()
            give_halo(conv, 1, core).start()

    def edges_came(conv):
        @pl.when(has_low)
        def _():
            past_up(conv).wait_recv()
            give_halo(conv, 0, 1 - core).wait_recv()

        @pl.when(has_high)
        def _():
            past_down(conv).wait_recv()
            give_halo(conv, 1, 1 - core).wait_recv()

    def convolve(conv, consume, between):
        def shift_rows(first, count):
            size = count * wide
            mine = pl.ds(first, count)

            def shift(n, _):
                flat = act[conv, n // 2, n % 2, mine].reshape(size, LANES).astype(F32)
                back = pltpu.roll(flat, 1, 0).astype(BF)
                ahead = pltpu.roll(flat, size - 1, 0).astype(BF)
                shifted[0, n, mine] = back.reshape(count, wide, LANES)
                shifted[1, n, mine] = ahead.reshape(count, wide, LANES)
                return 0

            lax.fori_loop(0, 2 * (chips + 1), shift, 0)

        def frame(q, g):
            first, second = GROUPS[g]

            def pair(load, r):
                if second == first + 1:
                    return load(first + r, 2).reshape(2 * wide, LANES)
                return jnp.concatenate(
                    [load(first + r, 1).reshape(wide, LANES), load(second + r, 1).reshape(wide, LANES)],
                    axis=0,
                )

            acc = jnp.zeros((2 * wide, chans), F32)
            for tap in range(3):
                n = 2 * q + core + tap
                pieces = []
                for r in range(3):
                    pieces.append(pair(lambda a, c: shifted[0, n, a : a + c], r))
                    pieces.append(pair(lambda a, c: act[conv, n // 2, n % 2, a : a + c], r))
                    pieces.append(pair(lambda a, c: shifted[1, n, a : a + c], r))
                acc = acc + jnp.dot(
                    jnp.concatenate(pieces, axis=1),
                    weights[conv, 9 * tap : 9 * tap + 9].reshape(9 * LANES, chans),
                    preferred_element_type=F32,
                )
            acc = acc.reshape(2, wide, chans)[:, :cols]
            work[first] = acc[0]
            work[second] = acc[1]

        def sum_row(r):
            row_copy(conv, 0, r).wait_recv()
            psend[conv, 2, r] = (kept[r] + precv[conv, 0, r].astype(F32)).astype(BF)
            row_copy(conv, 2, r).start()

        def plane_step(g, relay):
            def run(i, _):
                x = (chip + 1 - i // 2) % 2
                y = (chip // 2 + 1 - i % 2) % 2
                frame(2 * y + x, g)

                @pl.when(i == 0)
                def _():
                    for r in GROUPS[g]:
                        psend[conv, 0, r] = work[r].astype(BF)
                        row_copy(conv, 0, r).start()

                for i_of, parity in ((1, 0), (2, 1)):

                    @pl.when(i == i_of)
                    def _():
                        for r in GROUPS[g]:
                            if r % 2 == parity:
                                psend[conv, 1, r] = work[r].astype(BF)
                                row_copy(conv, 1, r).start()
                            else:
                                kept[r] = work[r]

                if relay:

                    @pl.when(i == 1)
                    def _():
                        pass_halo(conv)

                @pl.when(i == 2)
                def _():
                    for r in GROUPS[g]:
                        sum_row(r)

                return 0

            return run

        def finish(g):
            total_rows = []
            for r in GROUPS[g]:
                value = kept[r] if plane else work[r]
                for kind in range(1 if plane else 0, chips - 1):
                    if plane:
                        row_copy(conv, kind, r).wait_recv()
                    value = value + precv[conv, kind, r].astype(F32)
                total_rows.append(value)
            consume(g, jnp.concatenate(total_rows, axis=0))

        def step(d, _):
            for g in range(2):
                frame(peer(d), g)
            psend[conv, d - 1] = work[...].astype(BF)
            part_copy(conv, d).start()
            return 0

        shift_rows(1, rows)
        if plane:
            lax.fori_loop(0, 4, plane_step(0, True), 0)
            for r in GROUPS[0]:
                kept[r] = work[r]
            edges_came(conv)
            shift_rows(0, 1)
            shift_rows(rows + 1, 1)
            lax.fori_loop(0, 3, plane_step(1, False), 0)
            finish(0)
            frame(chip, 1)
            for r in GROUPS[1]:
                kept[r] = work[r]
            between()
            finish(1)
        else:
            pass_halo(conv)
            edges_came(conv)
            shift_rows(0, 1)
            shift_rows(rows + 1, 1)
            lax.fori_loop(1, chips, step, 0)
            for g in range(2):
                frame(chip, g)
            for d in range(1, chips):
                part_copy(conv, d).wait_recv()
            finish(0)
            between()
            finish(1)

    exchange(0)
    sent_weight(1, w2).start()
    local_weight(0, w1).wait()
    remote(w1, weight_slot(0, 1 - core), ws_sem.at[0], wr_sem.at[0], mate, z).wait_recv()

    def after_first(g, summed):
        hidden = summed + bias1[...].reshape(1, chans)
        put_stage(1, g, silu(normalize(hidden, gain2[...].reshape(1, chans))))
        for piece in (0,) if g == 0 else (1, 2):
            for d in range(1, chips):
                main_copy(1, d, piece).start()

    convolve(0, after_first, lambda: None)
    exchange(1)
    local_weight(1, w2).wait()
    remote(w2, weight_slot(1, 1 - core), ws_sem.at[1], wr_sem.at[1], mate, z).wait_recv()

    def right(b, h):
        return remote(
            held.at[b, h], held.at[b, h], xright_sem.at[b, h], xr_sem.at[b, h], t, z + 1
        )

    def left(b, h):
        return remote(
            held.at[b, h], held.at[b, h], xleft_sem.at[b, h], xr_sem.at[b, h], t, z - 1
        )

    def after_second(g, summed):
        conv_out = summed + bias2[...].reshape(1, chans)
        before = rows_of(video[...].astype(F32).reshape(rows, cols, chans), g)
        block = (before + conv_out).astype(BF)
        wider = block.astype(F32)
        for i, r in enumerate(GROUPS[g]):
            out[r] = wider[i * cols : (i + 1) * cols].astype(BF)
        held[z, g] = normalize(wider, gain3[...].reshape(1, chans)).astype(BF)

        @pl.when(has_high)
        def _():
            right(z, g).start()

        @pl.when(has_low)
        def _():
            left(z, g).start()

    def relay(k, g):
        @pl.when(z - k >= 0)
        def _():
            right(z - k, g).wait_recv()

            @pl.when(has_high)
            def _():
                right(z - k, g).start()

        @pl.when(z + k < bands)
        def _():
            left(z + k, g).wait_recv()

            @pl.when(has_low)
            def _():
                left(z + k, g).start()

    convolve(1, after_second, lambda: relay(1, 0))
    factor = 1.0 / (float(chans) ** 0.5)
    queries[...] = jnp.dot(held[z].reshape(cells, chans), wq[...], preferred_element_type=F32).astype(BF)
    top[...] = jnp.full(top.shape, -jnp.inf, F32)
    total[...] = jnp.zeros(total.shape, F32)
    accum[...] = jnp.zeros(accum.shape, F32)

    def attend(b):
        tokens = held[b].reshape(cells, chans)
        keys = jnp.dot(tokens, wk[...], preferred_element_type=F32).astype(BF)
        values = jnp.dot(tokens, wv[...], preferred_element_type=F32).astype(BF)
        scores = lax.dot_general(
            queries[...], keys, (((1,), (1,)), ((), ())), preferred_element_type=F32
        ) * factor
        before = top[...]
        now = jnp.maximum(before, jnp.max(scores, axis=1, keepdims=True))
        shrink = jnp.exp(before - now)
        expo = jnp.exp(scores - now)
        top[...] = now
        total[...] = total[...] * shrink + jnp.sum(expo, axis=1, keepdims=True)
        accum[...] = accum[...] * shrink + jnp.dot(
            expo.astype(BF), values, preferred_element_type=F32
        )

    attend(z)

    def ring(k, _):
        @pl.when(k > 1)
        def _():
            relay(k, 0)

        relay(k, 1)

        @pl.when(z - k >= 0)
        def _():
            attend(z - k)

        @pl.when(z + k < bands)
        def _():
            attend(z + k)

        return 0

    lax.fori_loop(1, bands, ring, 0)
    att = (accum[...] / total[...]).astype(BF)
    projected = jnp.dot(att, wo[...], preferred_element_type=F32)
    for g in range(2):
        for i, r in enumerate(GROUPS[g]):
            first = (2 * g + i) * cols
            out[r] = (out[r].astype(F32) + projected[first : first + cols]).astype(BF)

    def drain(b, _):
        @pl.when(jnp.logical_and(has_high, b <= z))
        def _():
            for h in range(2):
                right(b, h).wait_send()

        @pl.when(jnp.logical_and(has_low, b >= z))
        def _():
            for h in range(2):
                left(b, h).wait_send()

        return 0

    lax.fori_loop(0, bands, drain, 0)
    for conv, w in ((0, w1), (1, w2)):
        sent_weight(conv, w).wait_send()
        give_main(conv, core).wait_send()
        for d in range(1, chips):
            for piece in range(3):
                main_copy(conv, d, piece).wait_send()
            if plane:
                for r in range(rows):
                    row_copy(conv, d - 1, r).wait_send()
            else:
                part_copy(conv, d).wait_send()

        @pl.when(has_high)
        def _():
            halo_up(conv).wait_send()
            past_up(conv).wait_send()
            give_halo(conv, 1, core).wait_send()

        @pl.when(has_low)
        def _():
            halo_down(conv).wait_send()
            past_down(conv).wait_send()
            give_halo(conv, 0, core).wait_send()


def local(
    devices, bands,
    video, past_first, past_second, conv_first, bias_first, conv_second, bias_second,
    gain_first, gain_second, gain_attn, query_weight, key_weight, value_weight, out_weight,
):
    _, rows, cols, chans = video.shape
    chips = devices // 2
    share = chans // devices
    wide = (cols + 1 + 15) // 16 * 16
    cells = rows * cols
    direct = share % 16 == 0 and share < SLOT

    def weight_part(kernel_piece):
        flat = kernel_piece.reshape(27, share, chans)
        if direct:
            return flat
        return jnp.pad(flat, ((0, 0), (0, SLOT - share), (0, 0)))

    vmem = pl.BlockSpec(memory_space=pltpu.VMEM)
    hbm = pl.BlockSpec(memory_space=pl.ANY)
    dma = pltpu.SemaphoreType.DMA
    flops = 2 * 2 * cells * 27 * chans * chans + 4 * cells * cells * bands * chans
    encoded = pl.pallas_call(
        functools.partial(kernel, chips, bands, rows, cols, wide, share, direct),
        out_shape=jax.ShapeDtypeStruct((rows, cols, chans), BF),
        in_specs=[vmem] * 3 + [hbm] * 2 + [vmem] * 9,
        out_specs=vmem,
        scratch_shapes=[
            pltpu.VMEM((2, 27, 2, SLOT, chans), BF),
            pltpu.VMEM((2, chips, rows, wide, LANES), BF),
            pltpu.VMEM((2, chips + 1, 2, rows + 2, wide, LANES), BF),
            pltpu.VMEM((2, 2 * (chips + 1), rows + 2, wide, LANES), BF),
            pltpu.VMEM((2, chips - 1, rows, cols, chans), BF),
            pltpu.VMEM((2, chips - 1, rows, cols, chans), BF),
            pltpu.VMEM((rows, cols, chans), F32),
            pltpu.VMEM((rows, cols, chans), F32),
            pltpu.VMEM((bands, 2, cells // 2, chans), BF),
            pltpu.VMEM((cells, chans), BF),
            pltpu.VMEM((cells, 1), F32),
            pltpu.VMEM((cells, 1), F32),
            pltpu.VMEM((cells, chans), F32),
            dma((2,)), dma((2,)), dma((2,)),
            dma((2, chips, 3)), dma((2, chips, 3)),
            dma((2, 2)), dma((2, 2)), dma((2, 2)), dma((2, 2)),
            dma((2,)), dma((2,)), dma((2, 2)), dma((2, 2)),
            dma((2, chips, rows)), dma((2, chips, rows)),
            dma((bands, 2)), dma((bands, 2)), dma((bands, 2)),
        ],
        compiler_params=pltpu.CompilerParams(
            collective_id=0, has_side_effects=True, vmem_limit_bytes=56 * 1024 * 1024
        ),
        cost_estimate=pl.CostEstimate(
            flops=flops, bytes_accessed=8 * 1024 * 1024, transcendentals=cells * cells * bands
        ),
    )(
        video.reshape(cells, chans), past_first, past_second,
        weight_part(conv_first), weight_part(conv_second),
        bias_first, bias_second, gain_first, gain_second, gain_attn,
        query_weight, key_weight, value_weight, out_weight,
    )
    return encoded.reshape(video.shape)


def solution(mesh):
    return jax.shard_map(
        functools.partial(local, mesh.shape["tm"], mesh.shape["band"]),
        mesh=mesh,
        in_specs=(
            P("tm", "band", None, None),
            P(None, "band", None, None),
            P(None, "band", None, None),
            P(None, None, None, "tm", None),
            P(),
            P(None, None, None, "tm", None),
            P(),
            P(),
            P(),
            P(),
            P(),
            P(),
            P(),
            P(),
        ),
        out_specs=P("tm", "band", None, None),
        check_vma=False,
    )
```

```python
import functools

import jax
import jax.numpy as jnp
from jax import lax
from jax.experimental import pallas as pl
from jax.experimental.pallas import tpu as pltpu
from jax.sharding import PartitionSpec as P

MESH = pl.DeviceIdType.MESH
BF = jnp.bfloat16
F32 = jnp.float32
SLOT = 64
LANES = 2 * SLOT
GROUPS = ((1, 2), (0, 3))
PIECES = ((1, 2), (0, 1), (3, 1))


def normalize(v, gain):
    return v * lax.rsqrt(jnp.mean(v * v, axis=-1, keepdims=True) + 1e-06) * gain


def silu(v):
    return v / (1.0 + jnp.exp(-v))


def kernel(
    chips, bands, rows, cols, wide,
    share, direct,
    video, past1, past2, w1, w2, bias1, bias2, gain1, gain2, gain3,
    wq, wk, wv, wo, out,
    select, weights, stage, act, shifted, psend, precv, work, kept, held, queries, top, total, accum,
    wl_sem, ws_sem, wr_sem, ms_sem, mr_sem, hs_sem, hr_sem, qs_sem, qr_sem,
    fs_sem, fr_sem, gs_sem, gr_sem, ps_sem, pr_sem, xr_sem, xright_sem, xleft_sem,
):
    t = lax.axis_index("tm")
    z = lax.axis_index("band")
    chip = t // 2
    core = t % 2
    mate = t + 1 - 2 * core
    last = bands - 1
    plane = chips == 4
    cells = rows * cols
    chans = video.shape[1]
    has_low = z > 0
    has_high = z < last

    def remote(src, dst, send, recv, tm, band):
        return pltpu.make_async_remote_copy(
            src_ref=src, dst_ref=dst, send_sem=send, recv_sem=recv,
            device_id=(tm, band), device_id_type=MESH,
        )

    def peer(d):
        return lax.rem(chip + d, chips)

    barrier = pltpu.get_barrier_semaphore()
    pl.semaphore_signal(barrier, inc=1, device_id=(mate, z), device_id_type=MESH)
    for d in range(1, chips):
        pl.semaphore_signal(barrier, inc=1, device_id=(peer(d) * 2 + core, z), device_id_type=MESH)

    @pl.when(has_low)
    def _():
        pl.semaphore_signal(barrier, inc=1, device_id=(t, z - 1), device_id_type=MESH)

    @pl.when(has_high)
    def _():
        pl.semaphore_signal(barrier, inc=1, device_id=(t, z + 1), device_id_type=MESH)

    def weight_slot(conv, whose):
        slot = weights.at[conv, :, whose]
        return slot.at[:, pl.ds(0, share)] if direct else slot

    def local_weight(conv, w):
        return pltpu.make_async_copy(w, weight_slot(conv, core), wl_sem.at[conv])

    def sent_weight(conv, w):
        return remote(
            w, weight_slot(conv, core), ws_sem.at[conv], wr_sem.at[conv], mate, z
        )

    lane = lax.broadcasted_iota(jnp.int32, (chans, LANES), 1)
    upper = lane >= SLOT
    within = jnp.where(upper, lane - SLOT, lane)
    offset = lax.broadcasted_iota(jnp.int32, (chans, LANES), 0) - within
    offset = jnp.where(upper, offset - share, offset)
    offset = jnp.where(within < share, offset, -1)
    for q in range(chips + 1):
        owner = q if q < chips else chip
        select[:, q * LANES : (q + 1) * LANES] = jnp.where(
            offset == 2 * share * owner, 1.0, 0.0
        ).astype(BF)

    def spread_of(values, first, count):
        lead = values.shape[0] // cols
        cube = values.reshape(lead, cols, chans)
        cube = jnp.concatenate([cube, jnp.zeros((lead, wide - cols, chans), F32)], axis=1)
        flat = cube.reshape(lead * wide, chans).astype(BF)
        chosen = select[:, first * LANES : (first + count) * LANES]
        return jnp.dot(flat, chosen, preferred_element_type=F32).astype(BF)

    def put_stage(conv, g, values):
        spread = spread_of(values, 0, chips)
        for i, r in enumerate(GROUPS[g]):
            for q in range(chips):
                stage[conv, q, r] = spread[i * wide : (i + 1) * wide, q * LANES : (q + 1) * LANES]
            act[conv, chip + 1, core, r + 1] = stage[conv, chip, r]

    def rows_of(cube, g):
        first, second = GROUPS[g]
        return jnp.concatenate([cube[first], cube[second]], axis=0)

    def fill_past():
        for conv, past in ((0, past1), (1, past2)):
            for n in range(2):
                part = spread_of(past[n].reshape(cells, chans).astype(F32), chips, 1)
                act[conv, 0, n, 1 : rows + 1] = part.reshape(rows, wide, LANES)
            if direct:
                weights[conv, :, :, share:] = jnp.zeros((27, 2, SLOT - share, chans), BF)

            @pl.when(z == 0)
            def _():
                act[conv, :, :, 0:1] = jnp.zeros((chips + 1, 2, 1, wide, LANES), BF)

            @pl.when(z == last)
            def _():
                act[conv, :, :, rows + 1 : rows + 2] = jnp.zeros((chips + 1, 2, 1, wide, LANES), BF)

    local_weight(0, w1).start()
    local_weight(1, w2).start()
    vid = video[...].astype(F32).reshape(rows, cols, chans)
    for g in range(2):
        put_stage(0, g, silu(normalize(rows_of(vid, g), gain1[...].reshape(1, chans))))

    pl.semaphore_wait(
        barrier, chips + has_low.astype(jnp.int32) + has_high.astype(jnp.int32)
    )

    def main_copy(conv, d, piece):
        q = peer(d)
        first, count = PIECES[piece]
        return remote(
            stage.at[conv, q, pl.ds(first, count)],
            act.at[conv, chip + 1, core, pl.ds(first + 1, count)],
            ms_sem.at[conv, d, piece], mr_sem.at[conv, d, piece], q * 2 + core, z,
        )

    def main_came(conv, d, piece):
        source = lax.rem(chip + chips - d, chips)
        first, count = PIECES[piece]
        return remote(
            stage.at[conv, 0, pl.ds(first, count)],
            act.at[conv, source + 1, core, pl.ds(first + 1, count)],
            ms_sem.at[conv, d, piece], mr_sem.at[conv, d, piece], mate, z,
        )

    def past_up(conv):
        return remote(
            act.at[conv, 0, :, rows], act.at[conv, 0, :, 0],
            qs_sem.at[conv, 0], qr_sem.at[conv, 0], t, z + 1,
        )

    def past_down(conv):
        return remote(
            act.at[conv, 0, :, 1], act.at[conv, 0, :, rows + 1],
            qs_sem.at[conv, 1], qr_sem.at[conv, 1], t, z - 1,
        )

    def halo_up(conv):
        return remote(
            act.at[conv, pl.ds(1, chips), core, rows], act.at[conv, pl.ds(1, chips), core, 0],
            hs_sem.at[conv, 0], hr_sem.at[conv, 0], t, z + 1,
        )

    def halo_down(conv):
        return remote(
            act.at[conv, pl.ds(1, chips), core, 1],
            act.at[conv, pl.ds(1, chips), core, rows + 1],
            hs_sem.at[conv, 1], hr_sem.at[conv, 1], t, z - 1,
        )

    def give_main(conv, piece, whose):
        first, count = PIECES[piece]
        part = act.at[conv, pl.ds(1, chips), whose, pl.ds(first + 1, count)]
        return remote(part, part, fs_sem.at[conv, piece], fr_sem.at[conv, piece], mate, z)

    def give_halo(conv, side, whose):
        part = act.at[conv, pl.ds(1, chips), whose, side * (rows + 1)]
        return remote(part, part, gs_sem.at[conv, side], gr_sem.at[conv, side], mate, z)

    def part_copy(conv, d):
        return remote(
            psend.at[conv, d - 1], precv.at[conv, d - 1],
            ps_sem.at[conv, d - 1, 0], pr_sem.at[conv, d - 1, 0], peer(d) * 2 + core, z,
        )

    across = chip + 1 - 2 * (chip % 2)
    along = chip + 2 - 4 * (chip // 2)

    def row_copy(conv, kind, r):
        first, second = (across, along) if r % 2 == 0 else (along, across)
        target = second if kind == 2 else first
        return remote(
            psend.at[conv, kind, r], precv.at[conv, kind, r],
            ps_sem.at[conv, kind, r], pr_sem.at[conv, kind, r], target * 2 + core, z,
        )

    def exchange(conv):
        if conv == 0:
            sent_weight(0, w1).start()
            for piece in range(3):
                for d in range(1, chips):
                    main_copy(conv, d, piece).start()
            fill_past()
            for c in (0, 1):

                @pl.when(has_high)
                def _():
                    past_up(c).start()

                @pl.when(has_low)
                def _():
                    past_down(c).start()

        for piece in range(3):
            for d in range(1, chips):
                main_came(conv, d, piece).wait_recv()
            give_main(conv, piece, core).start()

        @pl.when(has_low)
        def _():
            halo_down(conv).start()

        @pl.when(has_high)
        def _():
            halo_up(conv).start()

        for piece in range(3):
            give_main(conv, piece, 1 - core).wait_recv()

    def pass_halo(conv):
        @pl.when(has_low)
        def _():
            halo_up(conv).wait_recv()
            give_halo(conv, 0, core).start()

        @pl.when(has_high)
        def _():
            halo_down(conv).wait_recv()
            give_halo(conv, 1, core).start()

    def edges_came(conv):
        @pl.when(has_low)
        def _():
            past_up(conv).wait_recv()
            give_halo(conv, 0, 1 - core).wait_recv()

        @pl.when(has_high)
        def _():
            past_down(conv).wait_recv()
            give_halo(conv, 1, 1 - core).wait_recv()

    def convolve(conv, consume, between):
        def shift_rows(first, count):
            size = count * wide
            mine = pl.ds(first, count)

            def shift(n, _):
                flat = act[conv, n // 2, n % 2, mine].reshape(size, LANES).astype(F32)
                back = pltpu.roll(flat, 1, 0).astype(BF)
                ahead = pltpu.roll(flat, size - 1, 0).astype(BF)
                shifted[0, n, mine] = back.reshape(count, wide, LANES)
                shifted[1, n, mine] = ahead.reshape(count, wide, LANES)
                return 0

            lax.fori_loop(0, 2 * (chips + 1), shift, 0)

        def frame(q, g):
            first, second = GROUPS[g]

            def pair(load, r):
                if second == first + 1:
                    return load(first + r, 2).reshape(2 * wide, LANES)
                return jnp.concatenate(
                    [load(first + r, 1).reshape(wide, LANES), load(second + r, 1).reshape(wide, LANES)],
                    axis=0,
                )

            acc = jnp.zeros((2 * wide, chans), F32)
            for tap in range(3):
                n = 2 * q + core + tap
                pieces = []
                for r in range(3):
                    pieces.append(pair(lambda a, c: shifted[0, n, a : a + c], r))
                    pieces.append(pair(lambda a, c: act[conv, n // 2, n % 2, a : a + c], r))
                    pieces.append(pair(lambda a, c: shifted[1, n, a : a + c], r))
                acc = acc + jnp.dot(
                    jnp.concatenate(pieces, axis=1),
                    weights[conv, 9 * tap : 9 * tap + 9].reshape(9 * LANES, chans),
                    preferred_element_type=F32,
                )
            acc = acc.reshape(2, wide, chans)[:, :cols]
            work[first] = acc[0]
            work[second] = acc[1]

        def sum_row(r):
            row_copy(conv, 0, r).wait_recv()
            psend[conv, 2, r] = (kept[r] + precv[conv, 0, r].astype(F32)).astype(BF)
            row_copy(conv, 2, r).start()

        def plane_step(g, relay):
            def run(i, _):
                x = (chip + 1 - i // 2) % 2
                y = (chip // 2 + 1 - i % 2) % 2
                frame(2 * y + x, g)

                @pl.when(i == 0)
                def _():
                    for r in GROUPS[g]:
                        psend[conv, 0, r] = work[r].astype(BF)
                        row_copy(conv, 0, r).start()

                for i_of, parity in ((1, 0), (2, 1)):

                    @pl.when(i == i_of)
                    def _():
                        for r in GROUPS[g]:
                            if r % 2 == parity:
                                psend[conv, 1, r] = work[r].astype(BF)
                                row_copy(conv, 1, r).start()
                            else:
                                kept[r] = work[r]

                if relay:

                    @pl.when(i == 1)
                    def _():
                        pass_halo(conv)

                @pl.when(i == 2)
                def _():
                    for r in GROUPS[g]:
                        sum_row(r)

                return 0

            return run

        def finish(g):
            total_rows = []
            for r in GROUPS[g]:
                value = kept[r] if plane else work[r]
                for kind in range(1 if plane else 0, chips - 1):
                    if plane:
                        row_copy(conv, kind, r).wait_recv()
                    value = value + precv[conv, kind, r].astype(F32)
                total_rows.append(value)
            consume(g, jnp.concatenate(total_rows, axis=0))

        def step(d, _):
            for g in range(2):
                frame(peer(d), g)
            psend[conv, d - 1] = work[...].astype(BF)
            part_copy(conv, d).start()
            return 0

        shift_rows(1, rows)
        if plane:
            lax.fori_loop(0, 4, plane_step(0, True), 0)
            for r in GROUPS[0]:
                kept[r] = work[r]
            edges_came(conv)
            shift_rows(0, 1)
            shift_rows(rows + 1, 1)
            lax.fori_loop(0, 3, plane_step(1, False), 0)
            finish(0)
            frame(chip, 1)
            for r in GROUPS[1]:
                kept[r] = work[r]
            between()
            finish(1)
        else:
            pass_halo(conv)
            edges_came(conv)
            shift_rows(0, 1)
            shift_rows(rows + 1, 1)
            lax.fori_loop(1, chips, step, 0)
            for g in range(2):
                frame(chip, g)
            for d in range(1, chips):
                part_copy(conv, d).wait_recv()
            finish(0)
            between()
            finish(1)

    exchange(0)
    sent_weight(1, w2).start()
    local_weight(0, w1).wait()
    remote(w1, weight_slot(0, 1 - core), ws_sem.at[0], wr_sem.at[0], mate, z).wait_recv()

    def after_first(g, summed):
        hidden = summed + bias1[...].reshape(1, chans)
        put_stage(1, g, silu(normalize(hidden, gain2[...].reshape(1, chans))))
        for piece in (0,) if g == 0 else (1, 2):
            for d in range(1, chips):
                main_copy(1, d, piece).start()

    convolve(0, after_first, lambda: None)
    exchange(1)
    local_weight(1, w2).wait()
    remote(w2, weight_slot(1, 1 - core), ws_sem.at[1], wr_sem.at[1], mate, z).wait_recv()

    def right(b, h):
        return remote(
            held.at[b, h], held.at[b, h], xright_sem.at[b, h], xr_sem.at[b, h], t, z + 1
        )

    def left(b, h):
        return remote(
            held.at[b, h], held.at[b, h], xleft_sem.at[b, h], xr_sem.at[b, h], t, z - 1
        )

    def after_second(g, summed):
        conv_out = summed + bias2[...].reshape(1, chans)
        before = rows_of(video[...].astype(F32).reshape(rows, cols, chans), g)
        block = (before + conv_out).astype(BF)
        wider = block.astype(F32)
        for i, r in enumerate(GROUPS[g]):
            out[r] = wider[i * cols : (i + 1) * cols].astype(BF)
        held[z, g] = normalize(wider, gain3[...].reshape(1, chans)).astype(BF)

        @pl.when(has_high)
        def _():
            right(z, g).start()

        @pl.when(has_low)
        def _():
            left(z, g).start()

    def relay(k, g):
        @pl.when(z - k >= 0)
        def _():
            right(z - k, g).wait_recv()

            @pl.when(has_high)
            def _():
                right(z - k, g).start()

        @pl.when(z + k < bands)
        def _():
            left(z + k, g).wait_recv()

            @pl.when(has_low)
            def _():
                left(z + k, g).start()

    convolve(1, after_second, lambda: relay(1, 0))
    factor = 1.0 / (float(chans) ** 0.5)
    queries[...] = jnp.dot(held[z].reshape(cells, chans), wq[...], preferred_element_type=F32).astype(BF)
    top[...] = jnp.full(top.shape, -jnp.inf, F32)
    total[...] = jnp.zeros(total.shape, F32)
    accum[...] = jnp.zeros(accum.shape, F32)

    def attend(b):
        tokens = held[b].reshape(cells, chans)
        keys = jnp.dot(tokens, wk[...], preferred_element_type=F32).astype(BF)
        values = jnp.dot(tokens, wv[...], preferred_element_type=F32).astype(BF)
        scores = lax.dot_general(
            queries[...], keys, (((1,), (1,)), ((), ())), preferred_element_type=F32
        ) * factor
        before = top[...]
        now = jnp.maximum(before, jnp.max(scores, axis=1, keepdims=True))
        shrink = jnp.exp(before - now)
        expo = jnp.exp(scores - now)
        top[...] = now
        total[...] = total[...] * shrink + jnp.sum(expo, axis=1, keepdims=True)
        accum[...] = accum[...] * shrink + jnp.dot(
            expo.astype(BF), values, preferred_element_type=F32
        )

    attend(z)

    def ring(k, _):
        @pl.when(k > 1)
        def _():
            relay(k, 0)

        relay(k, 1)

        @pl.when(z - k >= 0)
        def _():
            attend(z - k)

        @pl.when(z + k < bands)
        def _():
            attend(z + k)

        return 0

    lax.fori_loop(1, bands, ring, 0)
    att = (accum[...] / total[...]).astype(BF)
    projected = jnp.dot(att, wo[...], preferred_element_type=F32)
    for g in range(2):
        for i, r in enumerate(GROUPS[g]):
            first = (2 * g + i) * cols
            out[r] = (out[r].astype(F32) + projected[first : first + cols]).astype(BF)

    def drain(b, _):
        @pl.when(jnp.logical_and(has_high, b <= z))
        def _():
            for h in range(2):
                right(b, h).wait_send()

        @pl.when(jnp.logical_and(has_low, b >= z))
        def _():
            for h in range(2):
                left(b, h).wait_send()

        return 0

    lax.fori_loop(0, bands, drain, 0)
    for conv, w in ((0, w1), (1, w2)):
        sent_weight(conv, w).wait_send()
        for piece in range(3):
            give_main(conv, piece, core).wait_send()
        for d in range(1, chips):
            for piece in range(3):
                main_copy(conv, d, piece).wait_send()
            if plane:
                for r in range(rows):
                    row_copy(conv, d - 1, r).wait_send()
            else:
                part_copy(conv, d).wait_send()

        @pl.when(has_high)
        def _():
            halo_up(conv).wait_send()
            past_up(conv).wait_send()
            give_halo(conv, 1, core).wait_send()

        @pl.when(has_low)
        def _():
            halo_down(conv).wait_send()
            past_down(conv).wait_send()
            give_halo(conv, 0, core).wait_send()


def local(
    devices, bands,
    video, past_first, past_second, conv_first, bias_first, conv_second, bias_second,
    gain_first, gain_second, gain_attn, query_weight, key_weight, value_weight, out_weight,
):
    _, rows, cols, chans = video.shape
    chips = devices // 2
    share = chans // devices
    wide = (cols + 1 + 15) // 16 * 16
    cells = rows * cols
    direct = share % 16 == 0 and share < SLOT

    def weight_part(kernel_piece):
        flat = kernel_piece.reshape(27, share, chans)
        if direct:
            return flat
        return jnp.pad(flat, ((0, 0), (0, SLOT - share), (0, 0)))

    vmem = pl.BlockSpec(memory_space=pltpu.VMEM)
    hbm = pl.BlockSpec(memory_space=pl.ANY)
    dma = pltpu.SemaphoreType.DMA
    flops = 2 * 2 * cells * 27 * chans * chans + 4 * cells * cells * bands * chans
    encoded = pl.pallas_call(
        functools.partial(kernel, chips, bands, rows, cols, wide, share, direct),
        out_shape=jax.ShapeDtypeStruct((rows, cols, chans), BF),
        in_specs=[vmem] * 3 + [hbm] * 2 + [vmem] * 9,
        out_specs=vmem,
        scratch_shapes=[
            pltpu.VMEM((chans, (chips + 1) * LANES), BF),
            pltpu.VMEM((2, 27, 2, SLOT, chans), BF),
            pltpu.VMEM((2, chips, rows, wide, LANES), BF),
            pltpu.VMEM((2, chips + 1, 2, rows + 2, wide, LANES), BF),
            pltpu.VMEM((2, 2 * (chips + 1), rows + 2, wide, LANES), BF),
            pltpu.VMEM((2, chips - 1, rows, cols, chans), BF),
            pltpu.VMEM((2, chips - 1, rows, cols, chans), BF),
            pltpu.VMEM((rows, cols, chans), F32),
            pltpu.VMEM((rows, cols, chans), F32),
            pltpu.VMEM((bands, 2, cells // 2, chans), BF),
            pltpu.VMEM((cells, chans), BF),
            pltpu.VMEM((cells, 1), F32),
            pltpu.VMEM((cells, 1), F32),
            pltpu.VMEM((cells, chans), F32),
            dma((2,)), dma((2,)), dma((2,)),
            dma((2, chips, 3)), dma((2, chips, 3)),
            dma((2, 2)), dma((2, 2)), dma((2, 2)), dma((2, 2)),
            dma((2, 3)), dma((2, 3)), dma((2, 2)), dma((2, 2)),
            dma((2, chips, rows)), dma((2, chips, rows)),
            dma((bands, 2)), dma((bands, 2)), dma((bands, 2)),
        ],
        compiler_params=pltpu.CompilerParams(
            collective_id=0, has_side_effects=True, vmem_limit_bytes=56 * 1024 * 1024
        ),
        cost_estimate=pl.CostEstimate(
            flops=flops, bytes_accessed=8 * 1024 * 1024, transcendentals=cells * cells * bands
        ),
    )(
        video.reshape(cells, chans), past_first, past_second,
        weight_part(conv_first), weight_part(conv_second),
        bias_first, bias_second, gain_first, gain_second, gain_attn,
        query_weight, key_weight, value_weight, out_weight,
    )
    return encoded.reshape(video.shape)


def solution(mesh):
    return jax.shard_map(
        functools.partial(local, mesh.shape["tm"], mesh.shape["band"]),
        mesh=mesh,
        in_specs=(
            P("tm", "band", None, None),
            P(None, "band", None, None),
            P(None, "band", None, None),
            P(None, None, None, "tm", None),
            P(),
            P(None, None, None, "tm", None),
            P(),
            P(),
            P(),
            P(),
            P(),
            P(),
            P(),
            P(),
        ),
        out_specs=P("tm", "band", None, None),
        check_vma=False,
    )
```

```python
import functools

import jax
import jax.numpy as jnp
from jax import lax
from jax.experimental import pallas as pl
from jax.experimental.pallas import tpu as pltpu
from jax.sharding import PartitionSpec as P

MESH = pl.DeviceIdType.MESH
BF = jnp.bfloat16
F32 = jnp.float32
SLOT = 64
LANES = 2 * SLOT
GROUPS = ((1, 2), (0, 3))
PIECES = ((1, 2), (0, 1), (3, 1))


def normalize(v, gain):
    return v * lax.rsqrt(jnp.mean(v * v, axis=-1, keepdims=True) + 1e-06) * gain


def silu(v):
    return v / (1.0 + jnp.exp(-v))


def kernel(
    chips, bands, rows, cols, wide,
    share, direct,
    video, past1, past2, w1, w2, bias1, bias2, gain1, gain2, gain3,
    wq, wk, wv, wo, out,
    weights, stage, act, shifted, psend, precv, work, kept, held, queries, top, total, accum,
    wl_sem, ws_sem, wr_sem, ms_sem, mr_sem, hs_sem, hr_sem, qs_sem, qr_sem,
    fs_sem, fr_sem, gs_sem, gr_sem, ps_sem, pr_sem, xr_sem, xright_sem, xleft_sem,
):
    t = lax.axis_index("tm")
    z = lax.axis_index("band")
    chip = t // 2
    core = t % 2
    mate = t + 1 - 2 * core
    last = bands - 1
    plane = chips == 4
    cells = rows * cols
    chans = video.shape[1]
    has_low = z > 0
    has_high = z < last

    def remote(src, dst, send, recv, tm, band):
        return pltpu.make_async_remote_copy(
            src_ref=src, dst_ref=dst, send_sem=send, recv_sem=recv,
            device_id=(tm, band), device_id_type=MESH,
        )

    def peer(d):
        return lax.rem(chip + d, chips)

    barrier = pltpu.get_barrier_semaphore()
    pl.semaphore_signal(barrier, inc=1, device_id=(mate, z), device_id_type=MESH)
    for d in range(1, chips):
        pl.semaphore_signal(barrier, inc=1, device_id=(peer(d) * 2 + core, z), device_id_type=MESH)

    @pl.when(has_low)
    def _():
        pl.semaphore_signal(barrier, inc=1, device_id=(t, z - 1), device_id_type=MESH)

    @pl.when(has_high)
    def _():
        pl.semaphore_signal(barrier, inc=1, device_id=(t, z + 1), device_id_type=MESH)

    def weight_slot(conv, whose):
        slot = weights.at[conv, :, whose]
        return slot.at[:, pl.ds(0, share)] if direct else slot

    def local_weight(conv, w):
        return pltpu.make_async_copy(w, weight_slot(conv, core), wl_sem.at[conv])

    def sent_weight(conv, w):
        return remote(
            w, weight_slot(conv, core), ws_sem.at[conv], wr_sem.at[conv], mate, z
        )

    def spread_of(values, first, count):
        lead = values.shape[0] // cols
        cube = values.reshape(lead, cols, chans)
        cube = jnp.concatenate([cube, jnp.zeros((lead, wide - cols, chans), F32)], axis=1)
        flat = cube.reshape(lead * wide, chans).astype(BF)
        channel = lax.broadcasted_iota(jnp.int32, (chans, count * LANES), 0)
        lane = lax.broadcasted_iota(jnp.int32, (chans, count * LANES), 1)
        within = lane % SLOT
        source = (lane // SLOT + 2 * first) * share + within
        chosen = jnp.logical_and(channel == source, within < share)
        select = jnp.where(chosen, 1.0, 0.0).astype(BF)
        return jnp.dot(flat, select, preferred_element_type=F32).astype(BF)

    def put_stage(conv, g, values):
        spread = spread_of(values, 0, chips)
        for i, r in enumerate(GROUPS[g]):
            for q in range(chips):
                stage[conv, q, r] = spread[i * wide : (i + 1) * wide, q * LANES : (q + 1) * LANES]
            act[conv, chip + 1, core, r + 1] = stage[conv, chip, r]

    def rows_of(cube, g):
        first, second = GROUPS[g]
        return jnp.concatenate([cube[first], cube[second]], axis=0)

    def fill_past():
        for conv, past in ((0, past1), (1, past2)):
            for n in range(2):
                part = spread_of(past[n].reshape(cells, chans).astype(F32), chip, 1)
                act[conv, 0, n, 1 : rows + 1] = part.reshape(rows, wide, LANES)
            if direct:
                weights[conv, :, :, share:] = jnp.zeros((27, 2, SLOT - share, chans), BF)

            @pl.when(z == 0)
            def _():
                act[conv, :, :, 0:1] = jnp.zeros((chips + 1, 2, 1, wide, LANES), BF)

            @pl.when(z == last)
            def _():
                act[conv, :, :, rows + 1 : rows + 2] = jnp.zeros((chips + 1, 2, 1, wide, LANES), BF)

    local_weight(0, w1).start()
    local_weight(1, w2).start()
    vid = video[...].astype(F32).reshape(rows, cols, chans)
    for g in range(2):
        put_stage(0, g, silu(normalize(rows_of(vid, g), gain1[...].reshape(1, chans))))

    pl.semaphore_wait(
        barrier, chips + has_low.astype(jnp.int32) + has_high.astype(jnp.int32)
    )

    def main_copy(conv, d, piece):
        q = peer(d)
        first, count = PIECES[piece]
        return remote(
            stage.at[conv, q, pl.ds(first, count)],
            act.at[conv, chip + 1, core, pl.ds(first + 1, count)],
            ms_sem.at[conv, d, piece], mr_sem.at[conv, d, piece], q * 2 + core, z,
        )

    def main_came(conv, d, piece):
        source = lax.rem(chip + chips - d, chips)
        first, count = PIECES[piece]
        return remote(
            stage.at[conv, 0, pl.ds(first, count)],
            act.at[conv, source + 1, core, pl.ds(first + 1, count)],
            ms_sem.at[conv, d, piece], mr_sem.at[conv, d, piece], mate, z,
        )

    def past_up(conv):
        return remote(
            act.at[conv, 0, :, rows], act.at[conv, 0, :, 0],
            qs_sem.at[conv, 0], qr_sem.at[conv, 0], t, z + 1,
        )

    def past_down(conv):
        return remote(
            act.at[conv, 0, :, 1], act.at[conv, 0, :, rows + 1],
            qs_sem.at[conv, 1], qr_sem.at[conv, 1], t, z - 1,
        )

    def halo_up(conv):
        return remote(
            act.at[conv, pl.ds(1, chips), core, rows], act.at[conv, pl.ds(1, chips), core, 0],
            hs_sem.at[conv, 0], hr_sem.at[conv, 0], t, z + 1,
        )

    def halo_down(conv):
        return remote(
            act.at[conv, pl.ds(1, chips), core, 1],
            act.at[conv, pl.ds(1, chips), core, rows + 1],
            hs_sem.at[conv, 1], hr_sem.at[conv, 1], t, z - 1,
        )

    def give_main(conv, whose):
        part = act.at[conv, pl.ds(1, chips), whose, pl.ds(1, rows)]
        return remote(part, part, fs_sem.at[conv], fr_sem.at[conv], mate, z)

    def give_halo(conv, side, whose):
        part = act.at[conv, pl.ds(1, chips), whose, side * (rows + 1)]
        return remote(part, part, gs_sem.at[conv, side], gr_sem.at[conv, side], mate, z)

    def part_copy(conv, d):
        return remote(
            psend.at[conv, d - 1], precv.at[conv, d - 1],
            ps_sem.at[conv, d - 1, 0], pr_sem.at[conv, d - 1, 0], peer(d) * 2 + core, z,
        )

    across = chip + 1 - 2 * (chip % 2)
    along = chip + 2 - 4 * (chip // 2)

    def row_copy(conv, kind, r):
        first, second = (across, along) if r % 2 == 0 else (along, across)
        target = second if kind == 2 else first
        return remote(
            psend.at[conv, kind, r], precv.at[conv, kind, r],
            ps_sem.at[conv, kind, r], pr_sem.at[conv, kind, r], target * 2 + core, z,
        )

    def exchange(conv):
        if conv == 0:
            sent_weight(0, w1).start()
            for piece in range(3):
                for d in range(1, chips):
                    main_copy(conv, d, piece).start()
            fill_past()
            for c in (0, 1):

                @pl.when(has_high)
                def _():
                    past_up(c).start()

                @pl.when(has_low)
                def _():
                    past_down(c).start()

        for piece in (1, 2, 0):
            for d in range(1, chips):
                main_came(conv, d, piece).wait_recv()

        give_main(conv, core).start()

        @pl.when(has_low)
        def _():
            halo_down(conv).start()

        @pl.when(has_high)
        def _():
            halo_up(conv).start()

        give_main(conv, 1 - core).wait_recv()

    def pass_halo(conv):
        @pl.when(has_low)
        def _():
            halo_up(conv).wait_recv()
            give_halo(conv, 0, core).start()

        @pl.when(has_high)
        def _():
            halo_down(conv).wait_recv()
            give_halo(conv, 1, core).start()

    def edges_came(conv):
        @pl.when(has_low)
        def _():
            past_up(conv).wait_recv()
            give_halo(conv, 0, 1 - core).wait_recv()

        @pl.when(has_high)
        def _():
            past_down(conv).wait_recv()
            give_halo(conv, 1, 1 - core).wait_recv()

    def convolve(conv, consume, between):
        def shift_rows(first, count):
            size = count * wide
            mine = pl.ds(first, count)

            def shift(n, _):
                flat = act[conv, n // 2, n % 2, mine].reshape(size, LANES).astype(F32)
                back = pltpu.roll(flat, 1, 0).astype(BF)
                ahead = pltpu.roll(flat, size - 1, 0).astype(BF)
                shifted[0, n, mine] = back.reshape(count, wide, LANES)
                shifted[1, n, mine] = ahead.reshape(count, wide, LANES)
                return 0

            lax.fori_loop(0, 2 * (chips + 1), shift, 0)

        def frame(q, g):
            first, second = GROUPS[g]

            def pair(load, r):
                if second == first + 1:
                    return load(first + r, 2).reshape(2 * wide, LANES)
                return jnp.concatenate(
                    [load(first + r, 1).reshape(wide, LANES), load(second + r, 1).reshape(wide, LANES)],
                    axis=0,
                )

            acc = jnp.zeros((2 * wide, chans), F32)
            for tap in range(3):
                n = 2 * q + core + tap
                pieces = []
                for r in range(3):
                    pieces.append(pair(lambda a, c: shifted[0, n, a : a + c], r))
                    pieces.append(pair(lambda a, c: act[conv, n // 2, n % 2, a : a + c], r))
                    pieces.append(pair(lambda a, c: shifted[1, n, a : a + c], r))
                acc = acc + jnp.dot(
                    jnp.concatenate(pieces, axis=1),
                    weights[conv, 9 * tap : 9 * tap + 9].reshape(9 * LANES, chans),
                    preferred_element_type=F32,
                )
            acc = acc.reshape(2, wide, chans)[:, :cols]
            work[first] = acc[0]
            work[second] = acc[1]

        def sum_row(r):
            row_copy(conv, 0, r).wait_recv()
            psend[conv, 2, r] = (kept[r] + precv[conv, 0, r].astype(F32)).astype(BF)
            row_copy(conv, 2, r).start()

        def plane_step(g, relay):
            def run(i, _):
                x = (chip + 1 - i // 2) % 2
                y = (chip // 2 + 1 - i % 2) % 2
                frame(2 * y + x, g)

                @pl.when(i == 0)
                def _():
                    for r in GROUPS[g]:
                        psend[conv, 0, r] = work[r].astype(BF)
                        row_copy(conv, 0, r).start()

                for i_of, parity in ((1, 0), (2, 1)):

                    @pl.when(i == i_of)
                    def _():
                        for r in GROUPS[g]:
                            if r % 2 == parity:
                                psend[conv, 1, r] = work[r].astype(BF)
                                row_copy(conv, 1, r).start()
                            else:
                                kept[r] = work[r]

                if relay:

                    @pl.when(i == 1)
                    def _():
                        pass_halo(conv)

                @pl.when(i == 2)
                def _():
                    for r in GROUPS[g]:
                        sum_row(r)

                return 0

            return run

        def finish(g):
            total_rows = []
            for r in GROUPS[g]:
                value = kept[r] if plane else work[r]
                for kind in range(1 if plane else 0, chips - 1):
                    if plane:
                        row_copy(conv, kind, r).wait_recv()
                    value = value + precv[conv, kind, r].astype(F32)
                total_rows.append(value)
            consume(g, jnp.concatenate(total_rows, axis=0))

        def step(d, _):
            for g in range(2):
                frame(peer(d), g)
            psend[conv, d - 1] = work[...].astype(BF)
            part_copy(conv, d).start()
            return 0

        shift_rows(1, rows)
        if plane:
            lax.fori_loop(0, 4, plane_step(0, True), 0)
            for r in GROUPS[0]:
                kept[r] = work[r]
            edges_came(conv)
            shift_rows(0, 1)
            shift_rows(rows + 1, 1)
            lax.fori_loop(0, 2, plane_step(1, False), 0)
            finish(0)
            lax.fori_loop(2, 3, plane_step(1, False), 0)
            frame(chip, 1)
            for r in GROUPS[1]:
                kept[r] = work[r]
            between()
            finish(1)
        else:
            pass_halo(conv)
            edges_came(conv)
            shift_rows(0, 1)
            shift_rows(rows + 1, 1)
            lax.fori_loop(1, chips, step, 0)
            for g in range(2):
                frame(chip, g)
            for d in range(1, chips):
                part_copy(conv, d).wait_recv()
            finish(0)
            between()
            finish(1)

    exchange(0)
    sent_weight(1, w2).start()
    local_weight(0, w1).wait()
    remote(w1, weight_slot(0, 1 - core), ws_sem.at[0], wr_sem.at[0], mate, z).wait_recv()

    def after_first(g, summed):
        hidden = summed + bias1[...].reshape(1, chans)
        put_stage(1, g, silu(normalize(hidden, gain2[...].reshape(1, chans))))
        for piece in (0,) if g == 0 else (1, 2):
            for d in range(1, chips):
                main_copy(1, d, piece).start()

    convolve(0, after_first, lambda: None)
    exchange(1)
    local_weight(1, w2).wait()
    remote(w2, weight_slot(1, 1 - core), ws_sem.at[1], wr_sem.at[1], mate, z).wait_recv()

    def right(b, h):
        return remote(
            held.at[b, h], held.at[b, h], xright_sem.at[b, h], xr_sem.at[b, h], t, z + 1
        )

    def left(b, h):
        return remote(
            held.at[b, h], held.at[b, h], xleft_sem.at[b, h], xr_sem.at[b, h], t, z - 1
        )

    def after_second(g, summed):
        conv_out = summed + bias2[...].reshape(1, chans)
        before = rows_of(video[...].astype(F32).reshape(rows, cols, chans), g)
        block = (before + conv_out).astype(BF)
        wider = block.astype(F32)
        for i, r in enumerate(GROUPS[g]):
            out[r] = wider[i * cols : (i + 1) * cols].astype(BF)
        held[z, g] = normalize(wider, gain3[...].reshape(1, chans)).astype(BF)

        @pl.when(has_high)
        def _():
            right(z, g).start()

        @pl.when(has_low)
        def _():
            left(z, g).start()

    def relay(k, g):
        @pl.when(z - k >= 0)
        def _():
            right(z - k, g).wait_recv()

            @pl.when(has_high)
            def _():
                right(z - k, g).start()

        @pl.when(z + k < bands)
        def _():
            left(z + k, g).wait_recv()

            @pl.when(has_low)
            def _():
                left(z + k, g).start()

    convolve(1, after_second, lambda: relay(1, 0))
    factor = 1.0 / (float(chans) ** 0.5)
    queries[...] = jnp.dot(held[z].reshape(cells, chans), wq[...], preferred_element_type=F32).astype(BF)
    top[...] = jnp.full(top.shape, -jnp.inf, F32)
    total[...] = jnp.zeros(total.shape, F32)
    accum[...] = jnp.zeros(accum.shape, F32)

    def attend(b):
        tokens = held[b].reshape(cells, chans)
        keys = jnp.dot(tokens, wk[...], preferred_element_type=F32).astype(BF)
        values = jnp.dot(tokens, wv[...], preferred_element_type=F32).astype(BF)
        scores = lax.dot_general(
            queries[...], keys, (((1,), (1,)), ((), ())), preferred_element_type=F32
        ) * factor
        before = top[...]
        now = jnp.maximum(before, jnp.max(scores, axis=1, keepdims=True))
        shrink = jnp.exp(before - now)
        expo = jnp.exp(scores - now)
        top[...] = now
        total[...] = total[...] * shrink + jnp.sum(expo, axis=1, keepdims=True)
        accum[...] = accum[...] * shrink + jnp.dot(
            expo.astype(BF), values, preferred_element_type=F32
        )

    attend(z)

    def ring(k, _):
        @pl.when(k > 1)
        def _():
            relay(k, 0)

        relay(k, 1)

        @pl.when(z - k >= 0)
        def _():
            attend(z - k)

        @pl.when(z + k < bands)
        def _():
            attend(z + k)

        return 0

    lax.fori_loop(1, bands, ring, 0)
    att = (accum[...] / total[...]).astype(BF)
    projected = jnp.dot(att, wo[...], preferred_element_type=F32)
    for g in range(2):
        for i, r in enumerate(GROUPS[g]):
            first = (2 * g + i) * cols
            out[r] = (out[r].astype(F32) + projected[first : first + cols]).astype(BF)

    def drain(b, _):
        @pl.when(jnp.logical_and(has_high, b <= z))
        def _():
            for h in range(2):
                right(b, h).wait_send()

        @pl.when(jnp.logical_and(has_low, b >= z))
        def _():
            for h in range(2):
                left(b, h).wait_send()

        return 0

    lax.fori_loop(0, bands, drain, 0)
    for conv, w in ((0, w1), (1, w2)):
        sent_weight(conv, w).wait_send()
        give_main(conv, core).wait_send()
        for d in range(1, chips):
            for piece in range(3):
                main_copy(conv, d, piece).wait_send()
            if plane:
                for r in range(rows):
                    row_copy(conv, d - 1, r).wait_send()
            else:
                part_copy(conv, d).wait_send()

        @pl.when(has_high)
        def _():
            halo_up(conv).wait_send()
            past_up(conv).wait_send()
            give_halo(conv, 1, core).wait_send()

        @pl.when(has_low)
        def _():
            halo_down(conv).wait_send()
            past_down(conv).wait_send()
            give_halo(conv, 0, core).wait_send()


def local(
    devices, bands,
    video, past_first, past_second, conv_first, bias_first, conv_second, bias_second,
    gain_first, gain_second, gain_attn, query_weight, key_weight, value_weight, out_weight,
):
    _, rows, cols, chans = video.shape
    chips = devices // 2
    share = chans // devices
    wide = (cols + 1 + 15) // 16 * 16
    cells = rows * cols
    direct = share % 16 == 0 and share < SLOT

    def weight_part(kernel_piece):
        flat = kernel_piece.reshape(27, share, chans)
        if direct:
            return flat
        return jnp.pad(flat, ((0, 0), (0, SLOT - share), (0, 0)))

    vmem = pl.BlockSpec(memory_space=pltpu.VMEM)
    hbm = pl.BlockSpec(memory_space=pl.ANY)
    dma = pltpu.SemaphoreType.DMA
    flops = 2 * 2 * cells * 27 * chans * chans + 4 * cells * cells * bands * chans
    encoded = pl.pallas_call(
        functools.partial(kernel, chips, bands, rows, cols, wide, share, direct),
        out_shape=jax.ShapeDtypeStruct((rows, cols, chans), BF),
        in_specs=[vmem] * 3 + [hbm] * 2 + [vmem] * 9,
        out_specs=vmem,
        scratch_shapes=[
            pltpu.VMEM((2, 27, 2, SLOT, chans), BF),
            pltpu.VMEM((2, chips, rows, wide, LANES), BF),
            pltpu.VMEM((2, chips + 1, 2, rows + 2, wide, LANES), BF),
            pltpu.VMEM((2, 2 * (chips + 1), rows + 2, wide, LANES), BF),
            pltpu.VMEM((2, chips - 1, rows, cols, chans), BF),
            pltpu.VMEM((2, chips - 1, rows, cols, chans), BF),
            pltpu.VMEM((rows, cols, chans), F32),
            pltpu.VMEM((rows, cols, chans), F32),
            pltpu.VMEM((bands, 2, cells // 2, chans), BF),
            pltpu.VMEM((cells, chans), BF),
            pltpu.VMEM((cells, 1), F32),
            pltpu.VMEM((cells, 1), F32),
            pltpu.VMEM((cells, chans), F32),
            dma((2,)), dma((2,)), dma((2,)),
            dma((2, chips, 3)), dma((2, chips, 3)),
            dma((2, 2)), dma((2, 2)), dma((2, 2)), dma((2, 2)),
            dma((2,)), dma((2,)), dma((2, 2)), dma((2, 2)),
            dma((2, chips, rows)), dma((2, chips, rows)),
            dma((bands, 2)), dma((bands, 2)), dma((bands, 2)),
        ],
        compiler_params=pltpu.CompilerParams(
            collective_id=0, has_side_effects=True, vmem_limit_bytes=56 * 1024 * 1024
        ),
        cost_estimate=pl.CostEstimate(
            flops=flops, bytes_accessed=8 * 1024 * 1024, transcendentals=cells * cells * bands
        ),
    )(
        video.reshape(cells, chans), past_first, past_second,
        weight_part(conv_first), weight_part(conv_second),
        bias_first, bias_second, gain_first, gain_second, gain_attn,
        query_weight, key_weight, value_weight, out_weight,
    )
    return encoded.reshape(video.shape)


def solution(mesh):
    return jax.shard_map(
        functools.partial(local, mesh.shape["tm"], mesh.shape["band"]),
        mesh=mesh,
        in_specs=(
            P("tm", "band", None, None),
            P(None, "band", None, None),
            P(None, "band", None, None),
            P(None, None, None, "tm", None),
            P(),
            P(None, None, None, "tm", None),
            P(),
            P(),
            P(),
            P(),
            P(),
            P(),
            P(),
            P(),
        ),
        out_specs=P("tm", "band", None, None),
        check_vma=False,
    )
```
